32 devices in a mesh: branch: 2 (over x), dp: 16 (over z, y, core).
Axes of the slice: x: 2, y: 2, z: 4, core: 2. Of those that a mesh axis runs over, the one named last changes fastest.
Arguments:
- frames: bfloat16 [8192, 512], P(('branch', 'dp')), may hold values from -6 to 6
- lengths: int32 [32, 24], P(('branch', 'dp')), may hold values from 0 to 256, as said below
- cotangent: bfloat16 [8192, 512], P(('branch', 'dp')), may hold values from -6 to 6
- ffn_in: bfloat16 [2, 512, 2048], replicated, may hold values from -0.25 to 0.25
- ffn_in_bias: float32 [2, 2048], replicated, may hold values from -3 to 3
- ffn_out: bfloat16 [2, 2048, 512], replicated, may hold values from -0.125 to 0.125
- shared_gains: float32 [3, 512], replicated, may hold values from 0.25 to 1.75
- shared_shifts: float32 [6, 512], replicated, may hold values from -2 to 2
- merge_kernel: float32 [31, 1024], replicated, may hold values from -1 to 1
- merge_shift: float32 [1024], replicated, may hold values from -2 to 2
- merge_weight: bfloat16 [1024, 512], replicated, may hold values from -0.1875 to 0.1875
- attn_weights: bfloat16 [4, 512, 512], replicated, may hold values from -0.25 to 0.25
- attn_out: bfloat16 [512, 512], replicated, may hold values from -0.75 to 0.75
- attn_gain: float32 [512], replicated, may hold values from 0.25 to 1.75
- attn_vectors: float32 [6, 512], replicated, may hold values from -2 to 2
- mlp_in: bfloat16 [512, 3072], replicated, may hold values from -0.25 to 0.25
- mlp_in_bias: float32 [3072], replicated, may hold values from -3 to 3
- mlp_out: bfloat16 [1536, 512], replicated, may hold values from -0.15625 to 0.15625
- mlp_gain: float32 [512], replicated, may hold values from 0.25 to 1.75
- mlp_shifts: float32 [2, 512], replicated, may hold values from -2 to 2
- gate_gain: float32 [1536], replicated, may hold values from 0.25 to 1.75
- gate_shifts: float32 [2, 1536], replicated, may hold values from -2 to 2
- gate_kernel: float32 [31, 1536], replicated, may hold values from -1 to 1
Outputs:
- activations: bfloat16 [8192, 512], P(('branch', 'dp'))
- frame_grad: float32 [8192, 512], P(('branch', 'dp'))
- ffn_in_grad: float32 [2, 512, 2048], P(None, None, 'dp')
- ffn_in_bias_grad: float32 [2, 2048], P(None, 'dp')
- ffn_out_grad: float32 [2, 2048, 512], P(None, None, 'dp')
- shared_gains_grad: float32 [3, 512], P(None, 'dp')
- shared_shifts_grad: float32 [6, 512], P(None, 'dp')
- merge_kernel_grad: float32 [31, 1024], P(None, 'dp')
- merge_shift_grad: float32 [1024], P('dp')
- merge_weight_grad: float32 [1024, 512], P(None, 'dp')
- attn_weights_grad: float32 [4, 512, 512], P(None, None, 'dp')
- attn_out_grad: float32 [512, 512], P(None, 'dp')
- attn_gain_grad: float32 [512], P('dp')
- attn_vectors_grad: float32 [6, 512], P(None, 'dp')
- mlp_in_grad: float32 [512, 3072], P(None, 'dp')
- mlp_in_bias_grad: float32 [3072], P('dp')
- mlp_out_grad: float32 [1536, 512], P(None, 'dp')
- mlp_gain_grad: float32 [512], P('dp')
- mlp_shifts_grad: float32 [2, 512], P(None, 'dp')
- gate_gain_grad: float32 [1536], P('dp')
- gate_shifts_grad: float32 [2, 1536], P(None, 'dp')
- gate_kernel_grad: float32 [31, 1536], P(None, 'dp')
The draws below stay inside these ranges and needn't reach their ends.
Inputs may be any that keep to these rules, and one draw needn't show every extreme that they name: Each row holds the lengths of one block's utterances in order and sums to 256; a zero is an empty slot; in every draw some row is a single utterance of 256 frames.
All inputs are finite; a program needn't handle non-finite values.
Results may differ from the reference program's by a relative error of at most 0.019.
Values may be sent and summed in bfloat16 or wider, within the bound.
No kernel may reach another device: no remote copies, remote signals or barrier semaphores. Data moves between devices by JAX's collectives and lax.ppermute only.
A program may use at most 256 MiB of HBM per device.

```python
import math
import jax
import jax.numpy as jnp
from jax import lax

D = 512
HEADS = 8
FF = 2048
CG = 3072
KERNEL = 31
TOK_DEV = 256
SEGS = 24
TOKENS = 8192
DEVICES = 32


def draw_lengths(key, part):
    key = jax.random.fold_in(key, 7)
    cut_key, read_key, pick_key = jax.random.split(key, 3)
    shuffled = jax.vmap(lambda k: jax.random.permutation(k, TOK_DEV - 1))(jax.random.split(cut_key, DEVICES))
    cuts = jnp.sort(shuffled[:, :SEGS - 1] + 1, axis=1).astype(jnp.int32)
    edges = jnp.concatenate([jnp.zeros((DEVICES, 1), jnp.int32), cuts, jnp.full((DEVICES, 1), TOK_DEV, jnp.int32)], axis=1)
    commands = edges[:, 1:] - edges[:, :-1]
    reading = jax.random.randint(read_key, (DEVICES,), 0, 12) == 0
    chosen = jax.random.randint(pick_key, (), 0, DEVICES)
    reading = jnp.logical_or(reading, jnp.arange(DEVICES) == chosen)
    single = jnp.where(jnp.arange(SEGS) == 0, TOK_DEV, 0).astype(jnp.int32)
    return jnp.where(reading[:, None], single[None, :], commands).astype(jnp.int32)


def strengthened(values, key, source, target, blocks, factor):
    owner, partner = [(jnp.arange(values.shape[axis_at]) // (values.shape[axis_at] // blocks)).reshape([-1 if axis == axis_at else 1 for axis in range(values.ndim)]) for axis_at in (source, target)]
    chosen = jax.random.permutation(key, blocks)[partner]
    strong = (owner == chosen) | (owner == (partner + blocks // 2) % blocks)
    return jnp.where(strong, factor * values, values)


def block_levels(own_key, shape, cuts, smallest, top_value):
    def one(position, blocks):
        steps = jax.random.uniform(jax.random.fold_in(jax.random.fold_in(own_key, 6), position), (blocks,), jnp.float32, smallest / len(cuts), top_value / len(cuts))
        return jnp.repeat(jnp.exp(steps), shape[position] // blocks).reshape((-1,) + (1,) * (len(shape) - position - 1))

    loudness = one(*cuts[0])
    for cut in cuts[1:]:
        loudness = loudness * one(*cut)
    return loudness


def noise(own_key, dims, scale, most, cuts=(), kind=jnp.bfloat16):
    array = scale * jax.random.normal(own_key, dims, jnp.float32)
    if cuts:
        array = array * block_levels(own_key, dims, cuts, -0.22, 0.18)
    return jnp.clip(array, -most, most).astype(kind)


def noise_with(key, extent, scale, bound, shards, heavy, kind=jnp.bfloat16):
    drawn = scale * jax.random.normal(key, extent, jnp.float32)
    if shards:
        drawn = drawn * block_levels(key, extent, shards, -0.22, 0.18)
    return jnp.clip(strengthened(drawn, jax.random.fold_in(key, 3), *heavy), -bound, bound).astype(kind)


def setup_inputs(seed: int = 0) -> dict:
    key_list = jax.random.split(jax.random.key(seed), 24)
    return {
        "frames": noise(key_list[0], (TOKENS, D), 1.0, 6.0, ((0, 32),)),
        "lengths": draw_lengths(jax.random.fold_in(key_list[23], 71), 0),
        "cotangent": noise_with(key_list[2], (TOKENS, D), 1.0, 6.0, ((0, 32),), (0, 1, 32, 2.75)),
        "ffn_in": noise(key_list[3], (2, D, FF), D ** -0.5, 0.25),
        "ffn_in_bias": noise(key_list[4], (2, FF), 0.5, 3.0, (), jnp.float32),
        "ffn_out": noise(key_list[5], (2, FF, D), FF ** -0.5, 0.125),
        "shared_gains": jnp.clip(1.0 + 0.15 * jax.random.normal(key_list[6], (3, D), jnp.float32), 0.25, 1.75),
        "shared_shifts": noise(key_list[7], (6, D), 0.3, 2.0, (), jnp.float32),
        "merge_kernel": noise(key_list[8], (KERNEL, 2 * D), KERNEL ** -0.5, 1.0, (), jnp.float32),
        "merge_shift": noise(key_list[9], (2 * D,), 0.3, 2.0, (), jnp.float32),
        "merge_weight": noise(key_list[10], (2 * D, D), (2 * D) ** -0.5, 0.1875),
        "attn_weights": noise(key_list[11], (4, D, D), D ** -0.5, 0.25),
        "attn_out": noise(key_list[12], (D, D), (D // 8) ** -0.5, 0.75),
        "attn_gain": jnp.clip(1.0 + 0.15 * jax.random.normal(key_list[13], (D,), jnp.float32), 0.25, 1.75),
        "attn_vectors": noise(key_list[14], (6, D), 0.3, 2.0, (), jnp.float32),
        "mlp_in": noise(key_list[15], (D, CG), D ** -0.5, 0.25),
        "mlp_in_bias": noise(key_list[16], (CG,), 0.5, 3.0, (), jnp.float32),
        "mlp_out": noise(key_list[17], (CG // 2, D), (CG // 2) ** -0.5, 0.15625),
        "mlp_gain": jnp.clip(1.0 + 0.15 * jax.random.normal(key_list[18], (D,), jnp.float32), 0.25, 1.75),
        "mlp_shifts": noise(key_list[19], (2, D), 0.3, 2.0, (), jnp.float32),
        "gate_gain": jnp.clip(1.0 + 0.15 * jax.random.normal(key_list[20], (CG // 2,), jnp.float32), 0.25, 1.75),
        "gate_shifts": noise(key_list[21], (2, CG // 2), 0.3, 2.0, (), jnp.float32),
        "gate_kernel": noise(key_list[22], (KERNEL, CG // 2), KERNEL ** -0.5, 1.0, (), jnp.float32),
    }


epsilon = 1e-05

@jax.custom_vjp
def low(v):
    return lax.optimization_barrier(v.astype(jnp.bfloat16)).astype(jnp.float32)

@jax.custom_vjp
def low_back(v):
    return v

def low_keep(v):
    return (low(v), None)

def low_pass(kept, grad):
    return (grad,)

def back_keep(v):
    return (v, None)

def back_low(kept, grad):
    return (low(grad),)
low.defvjp(low_keep, low_pass)
low_back.defvjp(back_keep, back_low)

def layer_norm(values, scale_row, shift_row):
    center = values - lax.optimization_barrier(jnp.mean(values, axis=-1, keepdims=True))
    spread = lax.optimization_barrier(jnp.mean(center * center, axis=-1, keepdims=True))
    return center * lax.rsqrt(spread + epsilon) * scale_row + shift_row

def product(left, right, precision):
    return jnp.dot(left, right, precision=precision, preferred_element_type=jnp.float32)

def segment_numbers(sizes, frame_count):
    bounds = jnp.cumsum(sizes).astype(jnp.int32)
    places = jnp.arange(frame_count, dtype=jnp.int32)
    return lax.optimization_barrier(jnp.sum((bounds[None, :] <= places[:, None]).astype(jnp.int32), axis=1)).astype(jnp.int32)

def depthwise(values, kernel, segment):
    frame_count = values.shape[0]
    reach = kernel.shape[0] // 2
    padded = jnp.pad(values, ((reach, reach), (0, 0)))
    padded_ids = jnp.pad(segment, (reach, reach), constant_values=-1)
    total = jnp.zeros_like(values)
    for offset in range(kernel.shape[0]):
        same_seg = (padded_ids[offset:offset + frame_count] == segment)[:, None]
        total = total + jnp.where(same_seg, padded[offset:offset + frame_count], 0.0) * kernel[offset]
    return total

def feed_forward(values, scale_row, shift_row, w_first, b_first, w_second, b_second, precision):
    normed = low(layer_norm(values, scale_row, shift_row))
    hidden = low_back(product(normed, w_first, precision) + b_first)
    active = low(jax.nn.silu(hidden))
    return low_back(product(active, w_second, precision) + b_second)

def rel_table(frame_count, width):
    distance = (frame_count - 1 - jnp.arange(2 * frame_count - 1)).astype(jnp.float32)
    rates = jnp.exp(jnp.arange(0, width, 2).astype(jnp.float32) * (-math.log(10000.0) / width))
    angles = distance[:, None] * rates[None, :]
    return jnp.stack([jnp.sin(angles), jnp.cos(angles)], axis=-1).reshape(2 * frame_count - 1, width)

def rel_shift(full):
    frame_count, span = full.shape
    padded = jnp.pad(full, ((0, 0), (0, 1))).reshape(-1)
    taken = lax.slice(padded, (frame_count - 1,), (frame_count - 1 + frame_count * span,))
    return taken.reshape(frame_count, span)[:, :frame_count]

def attention_block(values, segment, scale_row, vectors, w_four, w_final, precision):
    frame_count, width = values.shape
    head_size = width // HEADS
    normed = low(layer_norm(values, scale_row, vectors[0]))
    query = low_back(product(normed, w_four[0], precision) + vectors[1])
    keys = low(low_back(product(normed, w_four[1], precision)))
    answers = low(low_back(product(normed, w_four[2], precision) + vectors[2]))
    table = low(rel_table(frame_count, width))
    placed = low(low_back(product(table, w_four[3], precision)))
    query_u = low(query + vectors[3])
    query_v = low(query + vectors[4])
    same_seg = segment[:, None] == segment[None, :]

    def per_head(pieces):
        with_u, with_v, head_keys, head_answers, head_places = pieces
        content = product(with_u, head_keys.T, precision)
        distant = rel_shift(product(with_v, head_places.T, precision))
        scores = low_back((content + distant) / math.sqrt(head_size))
        masked = jnp.where(same_seg, scores, -1e+30)
        weights = jnp.exp(masked - lax.optimization_barrier(jnp.max(masked, axis=1, keepdims=True)))
        probs = low(weights / lax.optimization_barrier(jnp.sum(weights, axis=1, keepdims=True)))
        return product(probs, head_answers, precision)

    def by_head(matrix):
        return matrix.reshape(matrix.shape[0], HEADS, head_size).transpose(1, 0, 2)
    context = lax.map(jax.checkpoint(per_head), (by_head(query_u), by_head(query_v), by_head(keys), by_head(answers), by_head(placed)))
    context = low(low_back(context.transpose(1, 0, 2).reshape(frame_count, width)))
    return low(low_back(product(context, w_final, precision) + vectors[5]))

def gating_block(values, segment, scale_row, shifts, w_first, b_first, w_second, gate_scale, gate_shift, kernel, precision):
    normed = low(layer_norm(values, scale_row, shifts[0]))
    hidden = low_back(product(normed, w_first, precision) + b_first)
    active = jax.nn.gelu(hidden, approximate=False)
    middle = active.shape[1] // 2
    mixed = depthwise(layer_norm(active[:, middle:], gate_scale, gate_shift[0]), kernel, segment) + gate_shift[1]
    gated = low(low_back(active[:, :middle] * mixed))
    return low(low_back(product(gated, w_second, precision) + shifts[1]))

def front_half(values, shared, precision):
    return values + 0.5 * feed_forward(values, shared[3][0], shared[4][0], shared[0][0], shared[1][0], shared[2][0], shared[4][1], precision)

def attention_branch(values, segment, attn, precision):
    return attention_block(values, segment, attn[2], attn[3], attn[0], attn[1], precision)

def gating_branch(values, segment, gating, precision):
    return gating_block(values, segment, gating[3], gating[4], gating[0], gating[1], gating[2], gating[5], gating[6], gating[7], precision)

def rear_half(first, attended, gated, segment, shared, precision):
    joined = jnp.concatenate([attended, gated], axis=1)
    summed = low(joined + depthwise(joined, shared[5], segment) + shared[6])
    second = first + low_back(product(summed, shared[7], precision) + shared[4][5])
    third = second + 0.5 * feed_forward(second, shared[3][1], shared[4][2], shared[0][1], shared[1][1], shared[2][1], shared[4][3], precision)
    return layer_norm(third, shared[3][2], shared[4][4])

def whole_block(values, segment, shared, attn, gating):
    precision = lax.Precision.HIGHEST
    first = front_half(values, shared, precision)
    sent = low(first)
    attended = attention_branch(sent, segment, attn, precision)
    gated = gating_branch(sent, segment, gating, precision)
    return rear_half(first, attended, gated, segment, shared, precision)

def reference(frames, lengths, cotangent, ffn_in, ffn_in_bias, ffn_out, shared_gains, shared_shifts, merge_kernel, merge_shift, merge_weight, attn_weights, attn_out, attn_gain, attn_vectors, mlp_in, mlp_in_bias, mlp_out, mlp_gain, mlp_shifts, gate_gain, gate_shifts, gate_kernel):
    shared = (ffn_in.astype(jnp.float32), ffn_in_bias, ffn_out.astype(jnp.float32), shared_gains, shared_shifts, merge_kernel, merge_shift, merge_weight.astype(jnp.float32))
    attn = (attn_weights.astype(jnp.float32), attn_out.astype(jnp.float32), attn_gain, attn_vectors)
    gating = (mlp_in.astype(jnp.float32), mlp_in_bias, mlp_out.astype(jnp.float32), mlp_gain, mlp_shifts, gate_gain, gate_shifts, gate_kernel)
    inputs = frames.astype(jnp.float32).reshape(DEVICES, TOK_DEV, D)
    incoming_all = cotangent.astype(jnp.float32).reshape(DEVICES, TOK_DEV, D)

    def one_block(totals, pieces):
        values, sizes, incoming = pieces
        segment = segment_numbers(sizes, TOK_DEV)
        result, pull = jax.vjp(lambda v, s, a, g: whole_block(v, segment, s, a, g), values, shared, attn, gating)
        g_values, g_shared, g_attn, g_gating = pull(incoming)
        totals = jax.tree.map(jnp.add, totals, (g_shared, g_attn, g_gating))
        return (totals, (result.astype(jnp.bfloat16), g_values))
    start = jax.tree.map(jnp.zeros_like, (shared, attn, gating))
    totals, (results, g_inputs) = lax.scan(one_block, start, (inputs, lengths, incoming_all))
    s_grad, a_grad, m_grad = totals
    return (results.reshape(TOKENS, D), g_inputs.reshape(TOKENS, D), s_grad[0], s_grad[1], s_grad[2], s_grad[3], s_grad[4], s_grad[5], s_grad[6], s_grad[7], a_grad[0], a_grad[1], a_grad[2], a_grad[3], m_grad[0], m_grad[1], m_grad[2], m_grad[3], m_grad[4], m_grad[5], m_grad[6], m_grad[7])
```

```python
import functools
import math

import jax
import jax.numpy as jnp
import numpy as np
from jax import lax
from jax.experimental import pallas as pl
from jax.experimental.pallas import tpu as pltpu
from jax.sharding import PartitionSpec as P

HEADS = 8
EPS = 1e-05
F32 = jnp.float32
BF16 = jnp.bfloat16
MIB = 1024 * 1024


def dot_nn(a, b):
    return lax.dot_general(a, b, (((1,), (0,)), ((), ())), preferred_element_type=F32)


def dot_nt(a, b):
    return lax.dot_general(a, b, (((1,), (1,)), ((), ())), preferred_element_type=F32)


def dot_tn(a, b):
    return lax.dot_general(a, b, (((0,), (0,)), ((), ())), preferred_element_type=F32)


def sigmoid(v):
    return 0.5 * jnp.tanh(0.5 * v) + 0.5


def normalize(v):
    center = v - jnp.mean(v, axis=-1, keepdims=True)
    spread = jnp.mean(center * center, axis=-1, keepdims=True)
    inverse = lax.rsqrt(spread + EPS)
    return center * inverse, inverse


def normalize_back(g_hat, hat, inverse):
    return inverse * (
        g_hat
        - jnp.mean(g_hat, axis=-1, keepdims=True)
        - hat * jnp.mean(g_hat * hat, axis=-1, keepdims=True)
    )


def rows_sum(v):
    return jnp.sum(v, axis=0, keepdims=True)


def tables(frame_count, width):
    distance = np.arange(frame_count - 1, -frame_count, -1).astype(np.float32)
    rates = np.exp(np.arange(0, width, 2).astype(np.float32) * np.float32(-math.log(10000.0) / width))
    angles = (distance[:, None] * rates[None, :].astype(np.float32)).astype(np.float64)
    rows = np.stack([np.sin(angles), np.cos(angles)], axis=-1).reshape(2 * frame_count - 1, width)
    zero = np.zeros((1, width))
    down = np.concatenate([rows, zero], axis=0).astype(np.float32)
    up = np.concatenate([rows[::-1], zero], axis=0).astype(np.float32)
    return jnp.asarray(down, BF16), jnp.asarray(up, BF16)


def fill_shifts(values_of, shifts_ref, width):
    rows = shifts_ref.shape[1]
    count = rows - 32

    def each(c, carry):
        lanes = pl.ds(pl.multiple_of(c * 128, 128), 128)
        shifts_ref[0, pl.ds(0, 16), lanes] = jnp.zeros((16, 128), F32)
        shifts_ref[0, pl.ds(16, count), lanes] = values_of(lanes)
        shifts_ref[0, pl.ds(16 + count, 16), lanes] = jnp.zeros((16, 128), F32)
        whole = shifts_ref[0, :, lanes]
        for s in range(1, 8):
            shifts_ref[s, :, lanes] = pltpu.roll(whole, rows - s, 0)
        return carry

    lax.fori_loop(0, width // 128, each, 0)


def fill_taps(kernel_ref, taps_ref, reverse, first_lane, width):
    taps = kernel_ref.shape[0]
    for t in range(taps):
        source = taps - 1 - t if reverse else t
        row = kernel_ref[pl.ds(source, 1), first_lane : first_lane + width]
        taps_ref[t, :, 0:width] = jnp.broadcast_to(row, (8, width))


def conv_rows(
    shifts_ref, taps_ref, low_ref, high_ref, first_lane, width, target_ref, values_ref=None, sums_ref=None, accumulate=False
):
    taps = taps_ref.shape[0]
    reach = taps // 2
    count = shifts_ref.shape[1] - 32
    row_tiles, lane_tiles = 4, 2
    row_blocks = count // (8 * row_tiles)

    def each(step, carry):
        block = step % row_blocks
        lane0 = pl.multiple_of((step // row_blocks) * (128 * lane_tiles), 128 * lane_tiles)
        row0 = pl.multiple_of(block * (8 * row_tiles), 8 * row_tiles)
        here = pl.ds(row0, 8 * row_tiles)
        near_lanes = pl.ds(lane0, 128 * lane_tiles)
        far_lanes = pl.ds(lane0 + first_lane, 128 * lane_tiles)
        shifts_here = shifts_ref.at[:, pl.ds(row0, 8 * row_tiles + 32), near_lanes]
        taps_here = taps_ref.at[:, :, near_lanes]
        low_here, high_here = low_ref.at[here, :], high_ref.at[here, :]
        rows = [pl.ds(8 * r, 8) for r in range(row_tiles)]
        lanes = [pl.ds(128 * l, 128) for l in range(lane_tiles)]
        low = [low_here[rows[r], :] for r in range(row_tiles)]
        high = [high_here[rows[r], :] for r in range(row_tiles)]
        total = [[None] * lane_tiles for r in range(row_tiles)]
        held = None
        if values_ref is not None:
            values_here = values_ref.at[here, far_lanes]
            sums_here = sums_ref.at[:, :, near_lanes]
            held = [[values_here[rows[r], lanes[l]] for l in range(lane_tiles)] for r in range(row_tiles)]
        for t in range(taps):
            away = t - reach
            start = 16 + away
            turn, base = start % 8, (start // 8) * 8
            tap = [taps_here[t, :, lanes[l]] for l in range(lane_tiles)]
            added = [None] * lane_tiles
            for r in range(row_tiles):
                same = None
                if away < 0:
                    same = low[r] <= away
                elif away > 0:
                    same = high[r] > away
                for l in range(lane_tiles):
                    near = shifts_here[turn, pl.ds(base + 8 * r, 8), lanes[l]]
                    if same is not None:
                        near = jnp.where(same, near, 0.0)
                    term = near * tap[l]
                    total[r][l] = term if total[r][l] is None else total[r][l] + term
                    if held is not None:
                        cross = near * held[r][l]
                        added[l] = cross if added[l] is None else added[l] + cross
            if held is not None:
                for l in range(lane_tiles):
                    sums_here[t, :, lanes[l]] += added[l]
        target_here = target_ref.at[here, far_lanes]
        for r in range(row_tiles):
            for l in range(lane_tiles):
                value = total[r][l]
                if accumulate:
                    value = target_here[rows[r], lanes[l]] + value
                target_here[rows[r], lanes[l]] = value
        return carry

    lax.fori_loop(0, row_blocks * (width // (128 * lane_tiles)), each, 0, unroll=2)


def tap_sums(sums_ref, out_ref):
    taps = sums_ref.shape[0]
    for t in range(taps):
        out_ref[pl.ds(taps - 1 - t, 1), :] = rows_sum(sums_ref[t])


def place(exact):
    if not exact:
        return None
    dp = lax.axis_index("dp")
    return lax.axis_index("branch"), (dp >> 2) & 3, (dp >> 1) & 1, dp & 1


def emit(here, keep, send, rows, value_of, per, parts):
    for group in range(8):
        z, y = group // 2, group % 2
        for side, ref in ((0, keep), (1, send)):
            for part, first, count, half, row in parts:
                if here is None:
                    base = ((half * 2 + y) * 4 + z) * rows + row
                    begin = (2 * group + side) * per + first
                else:
                    cx, cz, cy, core = here
                    base = pl.multiple_of((((half ^ cx) * 2 + (y ^ cy)) * 4 + (z ^ cz)) * rows + row, 16)
                    begin = pl.multiple_of((2 * group + (core ^ side)) * per + first, 16)
                ref[pl.ds(base, count), :] = value_of(begin, count, part)


def add_rows(target, row, count, *terms):
    step = max(step for step in range(16, 257, 16) if count % step == 0)

    def each(at, carry):
        away = pl.multiple_of(at * step, 16)
        values = [ref[pl.ds(away + first, step), :] for ref, first in terms]
        if len(values) == 2:
            total = values[0] + values[1]
        else:
            total = functools.reduce(jnp.add, [value.astype(F32) for value in values]).astype(BF16)
        target[pl.ds(away + row, step), :] = total
        return carry

    lax.fori_loop(0, count // step, each, 0)


def front_part(io, frames, lengths, gains, shifts, b1, w1, w2, y1_o, p_o, low_o, high_o):
    count = frames.shape[0]
    x = frames[...].astype(F32)
    hat, _ = normalize(x)
    n = (hat * gains[0:1, :] + shifts[0:1, :]).astype(BF16)

    where = lax.broadcasted_iota(jnp.int32, (count, 128), 0)
    begin = jnp.zeros((count, 128), jnp.int32)
    end = jnp.full((count, 128), count, jnp.int32)
    bound = jnp.int32(0)
    for s in range(lengths.shape[1]):
        bound = bound + lengths[0, s]
        before = bound <= where
        begin = jnp.where(before, bound, begin)
        end = jnp.where(before, end, jnp.minimum(end, bound))
    low_o[...] = begin - where
    high_o[...] = end - where
    io.ship("low", "high")
    io.wait("w1_0", "w2_0")
    total = jnp.zeros(x.shape, F32)
    for c in range(w1.shape[1] // 512):
        cols = slice(c * 512, (c + 1) * 512)
        p = dot_nn(n, w1[:, cols]) + b1[0:1, cols]
        p_o[:, cols] = p
        a = (p * sigmoid(p)).astype(BF16)
        total = total + dot_nn(a, w2[cols, :])
    io.ship("p1")
    y1_o[...] = x + 0.5 * (total + shifts[1:2, :])
    io.ship("y1")


def head_mask(which, rows):
    lane = lax.broadcasted_iota(jnp.int32, (rows, 128), 1)
    return (lane < 64) if which == 0 else (lane >= 64)


def attend_part(
    io, y1, table, w4, wo, gain, vec, low, high,
    att_o, na_o, qu_o, qv_o, k_o, v_o, probs_o, ctx_o, pk, bias,
):
    count = y1.shape[0]
    u = y1[...].astype(BF16).astype(F32)
    hat, _ = normalize(u)
    na = (hat * gain[...] + vec[0:1, :]).astype(BF16)
    na_o[...] = na
    io.wait("w4", "table")
    q = dot_nn(na, w4[0]) + vec[1:2, :]
    qu_o[...] = (q + vec[3:4, :]).astype(BF16)
    qv_o[...] = (q + vec[4:5, :]).astype(BF16)
    k_o[...] = dot_nn(na, w4[1]).astype(BF16)
    v_o[...] = (dot_nn(na, w4[2]) + vec[2:3, :]).astype(BF16)
    pk[...] = dot_nn(table[...], w4[3]).astype(BF16)
    row = lax.broadcasted_iota(jnp.int32, (count, 128), 0)
    lane = lax.broadcasted_iota(jnp.int32, (count, 128), 1)
    for c in range(count // 128):
        away = lane + c * 128 - row
        same = (low[...] <= away) & (high[...] > away)
        bias[:, c * 128 : (c + 1) * 128] = jnp.where(same, 0.0, -1e30)
    io.ship("na", "qu", "qv", "k", "v")
    scale = 1.0 / math.sqrt(512 // HEADS)
    for pair in range(HEADS // 2):
        cols = slice(pair * 128, (pair + 1) * 128)
        outs = []
        for h in range(2):
            mask = head_mask(h, count)
            qu = jnp.where(mask, qu_o[:, cols], jnp.zeros((), BF16))
            qv = jnp.where(mask, qv_o[:, cols], jnp.zeros((), BF16))
            content = dot_nt(qu, k_o[:, cols])
            distant = dot_nt(qv, pk[:, cols])
            distant = pltpu.roll(distant, count + 1, 1, stride=1, stride_axis=0)[:, :count]
            scores = (content + distant) * scale + bias[...]
            weights = jnp.exp(scores - jnp.max(scores, axis=1, keepdims=True))
            probs = weights * (1.0 / jnp.sum(weights, axis=1, keepdims=True))
            probs = probs.astype(BF16)
            probs_o[2 * pair + h] = probs
            outs.append(dot_nn(probs, v_o[:, cols]))
        ctx_o[:, cols] = jnp.where(head_mask(0, count), outs[0], outs[1]).astype(BF16)
    io.ship("probs", "ctx")
    io.wait("wo")
    att_o[...] = (dot_nn(ctx_o[...], wo[...]) + vec[5:6, :]).astype(BF16)


def gate_part(
    io, y1, w_in, b_in, w_out, gain, shifts, g_gain, g_shifts, taps, low, high,
    mix_o, nm_o, slope_o, zr_o, c_o, hat_o, inv_o, gated, zg, moved, spread_taps,
):
    half = zr_o.shape[1]
    u = y1[...].astype(BF16).astype(F32)
    hat, _ = normalize(u)
    nm = (hat * gain[...] + shifts[0:1, :]).astype(BF16)
    nm_o[...] = nm
    io.wait("w_in")
    for c in range(w_in.shape[1] // 512):
        cols = slice(c * 512, (c + 1) * 512)
        h = dot_nn(nm, w_in[:, cols]) + b_in[:, cols]
        cdf = 0.5 + 0.5 * lax.erf(h * math.sqrt(0.5))
        z = h * cdf
        slope = cdf + h * (jnp.exp(-0.5 * h * h) * (1.0 / math.sqrt(2.0 * math.pi)))
        slope_o[:, cols] = slope.astype(BF16)
        if c < half // 512:
            zr_o[:, cols] = z.astype(BF16)
        else:
            zg[:, c * 512 - half : (c + 1) * 512 - half] = z
    io.ship("nm", "slope", "zr")
    v = zg[...]
    center = v - jnp.mean(v, axis=-1, keepdims=True)
    inverse = lax.rsqrt(jnp.mean(center * center, axis=-1, keepdims=True) + EPS)
    zg[...] = center * inverse
    inv_o[...] = jnp.broadcast_to(inverse, inv_o.shape)
    hat_o[...] = zg[...].astype(BF16)
    io.ship("hat", "inv")

    width = moved.shape[2]
    for first in range(0, half, width):

        def line(lanes, first=first):
            far = pl.ds(lanes.start + first, lanes.size)
            return zg[:, far] * g_gain[:, far] + g_shifts[0:1, far]

        fill_shifts(line, moved, width)
        fill_taps(taps, spread_taps, False, first, width)
        conv_rows(moved, spread_taps, low, high, first, width, zg)
    for c in range(half // 512):
        cols = slice(c * 512, (c + 1) * 512)
        mixed = zg[:, cols] + g_shifts[1:2, cols]
        c_o[:, cols] = mixed.astype(BF16)
        gated[:, cols] = (zr_o[:, cols].astype(F32) * mixed).astype(BF16)
    io.ship("c")
    io.wait("w_out")
    mix_o[...] = (dot_nn(gated[...], w_out[...]) + shifts[1:2, :]).astype(BF16)


def rear_part(
    exact, io, y1, att, mix, cot, w1, b1, w2, gains, shifts, taps, m_shift, wm, low, high,
    act_o, g2_o, e, joined, keep, send, gb1_o, ggain_o, gshift_o,
    moved, spread_taps, p, a, dw,
):
    width = joined.shape[1]
    joined[:, :512] = att[...].astype(F32)
    joined[:, 512:] = mix[...].astype(F32)
    io.ship("joined")

    for first in range(0, width, 512):
        fill_shifts(lambda lanes: joined[:, pl.ds(lanes.start + first, lanes.size)], moved, 512)
        fill_taps(taps, spread_taps, False, first, 512)
        conv_rows(moved, spread_taps, low, high, first, 512, p)
    e[...] = (joined[...] + p[:, :width] + m_shift[...]).astype(BF16)
    io.ship("e")
    io.wait("wm")
    y2 = y1[...] + dot_nn(e[...], wm[...]) + shifts[5:6, :]
    hat2, inv2 = normalize(y2)
    n = (hat2 * gains[1:2, :] + shifts[2:3, :]).astype(BF16)
    io.wait("w1_1", "w2_1", "cot")
    total = jnp.zeros(y2.shape, F32)
    for c in range(w1.shape[1] // 512):
        cols = slice(c * 512, (c + 1) * 512)
        h = dot_nn(n, w1[:, cols]) + b1[1:2, cols]
        p[:, cols] = h
        act = (h * sigmoid(h)).astype(BF16)
        a[:, cols] = act
        total = total + dot_nn(act, w2[cols, :])
    y3 = y2 + 0.5 * (total + shifts[3:4, :])
    hat3, inv3 = normalize(y3)
    act_o[...] = (hat3 * gains[2:3, :] + shifts[4:5, :]).astype(BF16)
    io.ship("act")

    g = cot[...].astype(F32)
    ggain_o[1:2, :] = rows_sum(g * hat3)
    gshift_o[2:3, :] = rows_sum(g)
    g3 = normalize_back(g * gains[2:3, :], hat3, inv3)
    gf = (0.5 * g3).astype(BF16)
    gshift_o[1:2, :] = rows_sum(gf.astype(F32))
    g_hid = hidden_back(functools.partial(emit, place(exact), keep, send, 128), n, gf, p, a, w1, w2, gb1_o, dw)
    io.ship("send_r", "keep_r")
    ggain_o[0:1, :] = rows_sum(g_hid * hat2)
    gshift_o[0:1, :] = rows_sum(g_hid)
    g2 = g3 + normalize_back(g_hid * gains[1:2, :], hat2, inv2)
    g2_o[...] = g2
    gshift_o[3:4, :] = rows_sum(g2.astype(BF16).astype(F32))


FORWARD_IN = (
    "frames", "lengths", "cot", "w1_0", "w1_1", "b1", "w2_0", "w2_1", "gains", "shifts", "m_taps", "m_shift", "wm",
    "w4", "wo", "a_gain", "vec", "w_in", "b_in", "w_out", "m_gain", "m_shifts", "g_gain", "g_shifts", "g_taps",
    "table",
)
FORWARD_OUT = (
    "y1", "p1", "low", "high", "na", "qu", "qv", "k", "v", "probs", "ctx", "nm", "slope", "zr", "c", "hat", "inv",
    "act", "g2", "e", "joined", "keep_r", "send_r", "gb1", "ggain", "gshift", "a_gain_row", "m_gain_row",
    "g_gain_row",
)
FORWARD_LATER = (
    "w1_0", "w2_0", "a_gain", "vec", "m_shift", "b_in", "m_gain", "m_shifts", "g_gain", "g_shifts", "g_taps",
    "m_taps", "w4", "table", "wo", "w_in", "w_out", "wm", "cot", "w1_1", "w2_1",
)


class Named:
    def __init__(self, io):
        self.io = io

    def wait(self, *names):
        self.io.wait(*[FORWARD_IN.index(name) for name in names])

    def ship(self, *names):
        self.io.ship(*[FORWARD_OUT.index(name) for name in names])


def forward_kernel(exact, io, *refs):
    i = dict(zip(FORWARD_IN, refs))
    o = dict(zip(FORWARD_OUT, refs[len(FORWARD_IN) :]))
    (
        att, mix, pk, bias, gated, zg, moved, spread_taps, p, a, dw, m_shift, b_in,
    ) = refs[len(FORWARD_IN) + len(FORWARD_OUT) :]
    io = Named(io)
    front_part(
        io, i["frames"], i["lengths"], i["gains"], i["shifts"], i["b1"], i["w1_0"], i["w2_0"],
        o["y1"], o["p1"], o["low"], o["high"],
    )
    io.wait("a_gain", "vec", "m_shift", "b_in", "m_gain", "m_shifts", "g_gain", "g_shifts", "g_taps", "m_taps")
    for source, target in (
        ("a_gain", o["a_gain_row"]), ("m_gain", o["m_gain_row"]), ("g_gain", o["g_gain_row"]), ("m_shift", m_shift),
        ("b_in", b_in),
    ):
        target[...] = i[source][...].reshape(target.shape)
    io.ship("a_gain_row", "m_gain_row", "g_gain_row")
    attend_part(
        io, o["y1"], i["table"], i["w4"], i["wo"], o["a_gain_row"], i["vec"], o["low"], o["high"],
        att, o["na"], o["qu"], o["qv"], o["k"], o["v"], o["probs"], o["ctx"], pk, bias,
    )
    gate_part(
        io, o["y1"], i["w_in"], b_in, i["w_out"], o["m_gain_row"], i["m_shifts"], o["g_gain_row"], i["g_shifts"],
        i["g_taps"], o["low"], o["high"],
        mix, o["nm"], o["slope"], o["zr"], o["c"], o["hat"], o["inv"], gated, zg, moved, spread_taps,
    )
    rear_part(
        exact, io, o["y1"], att, mix, i["cot"], i["w1_1"], i["b1"], i["w2_1"], i["gains"], i["shifts"], i["m_taps"],
        m_shift, i["wm"], o["low"], o["high"],
        o["act"], o["g2"], o["e"], o["joined"], o["keep_r"], o["send_r"], o["gb1"], o["ggain"], o["gshift"],
        moved, spread_taps, p, a, dw,
    )


def merge_back_kernel(
    io, g2, joined, taps, wm, low, high, gatt_o, gmix_o, gtaps_o, gmshift_o, moved, spread_taps, sums, ge,
):
    width = joined.shape[1]
    fill_taps(taps, spread_taps, True, 0, width)
    sums[...] = jnp.zeros(sums.shape, F32)
    io.wait(0, 3)
    value = dot_nt(g2[...].astype(BF16), wm[...])
    gmshift_o[...] = rows_sum(value)
    ge[...] = value
    fill_shifts(lambda lanes: ge[:, lanes], moved, width)
    io.wait(1, 4, 5)

    conv_rows(moved, spread_taps, low, high, 0, width, ge, joined, sums, True)
    tap_sums(sums, gtaps_o)
    gatt_o[...] = ge[:, :512].astype(BF16)
    gmix_o[...] = ge[:, 512:].astype(BF16)


def hidden_back(put, n, gf, p, a, w1, w2, gb1_o, dw):
    hidden = p.shape[1]
    turned = gf.T
    for c in range(hidden // 512):
        cols = slice(c * 512, (c + 1) * 512)
        dw[:, cols] = dot_nn(turned, a[:, cols]).astype(BF16)
    put(
        lambda start, count, part: dw[pl.ds(start, count), part * 512 : (part + 1) * 512],
        32, [(part, 0, 32, 1, 32 * part) for part in range(hidden // 512)],
    )
    total = jnp.zeros(n.shape, F32)
    for c in range(hidden // 512):
        cols = slice(c * 512, (c + 1) * 512)
        h = p[:, cols]
        s = sigmoid(h)
        ga = dot_nt(gf, w2[cols, :])
        gp = (ga * (s * (1.0 + h * (1.0 - s)))).astype(BF16)
        gb1_o[:, cols] = rows_sum(gp.astype(F32))
        a[:, cols] = gp
        total = total + dot_nt(gp, w1[:, cols])
    turned = n.T
    for c in range(hidden // 512):
        cols = slice(c * 512, (c + 1) * 512)
        dw[:, cols] = dot_nn(turned, a[:, cols]).astype(BF16)

    def quarters(start, count, part):
        lanes = start if isinstance(start, int) else pl.multiple_of(start, 128)
        return jnp.concatenate([dw[pl.ds(128 * q, count), pl.ds(lanes, 128)] for q in range(4)], axis=1)

    put(quarters, 128, [(0, 0, 128, 0, 0)])
    return total


def gate_back_first_kernel(
    io, gmix, slope, zr, c, hat, w_out, g_gain, g_shifts, taps, low, high,
    gh, gc_o, gl_o, gbin_o, ggshift_o, gtaps_o, gmshift_o, moved, spread_taps, sums, line,
):
    half = zr.shape[1]
    part_width = line.shape[1]
    fill_taps(taps, spread_taps, True, 0, part_width)
    sums[...] = jnp.zeros(sums.shape, F32)
    io.wait(0, 1, 2, 3, 5)
    gm = gmix[...]
    gmshift_o[...] = rows_sum(gm.astype(F32))
    for k in range(half // 256):
        cols = slice(k * 256, (k + 1) * 256)
        gg = dot_nt(gm, w_out[cols, :]).astype(BF16).astype(F32)
        gzr = gg * c[:, cols].astype(F32)
        gc = gg * zr[:, cols].astype(F32)
        part = (gzr * slope[:, cols].astype(F32)).astype(BF16)
        gh[:, cols] = part
        gbin_o[:, cols] = rows_sum(part.astype(F32))
        ggshift_o[:, cols] = rows_sum(gc)
        if k * 256 < part_width:
            moved[0, pl.ds(16, 256), cols] = gc
        else:
            gc_o[:, k * 256 - part_width : (k + 1) * 256 - part_width] = gc
    io.ship(0, 1, 3, 4, 6)
    io.wait(4)
    line[...] = hat[:, :part_width].astype(F32) * g_gain[:, :part_width] + g_shifts[0:1, :part_width]
    fill_shifts(lambda lanes: moved[0, pl.ds(16, 256), lanes], moved, part_width)

    conv_rows(moved, spread_taps, low, high, 0, part_width, gl_o, line, sums)
    tap_sums(sums, gtaps_o)


def gate_back_second_kernel(
    io, gc, gl_first, slope, hat, inv, g_gain, g_shifts, taps, low, high, y1, gh_first, w_in, gain,
    gu_o, gh, gbin_o, gggain_o, ggshift_o, gtaps_o, ggain_o, gshift_o, moved, spread_taps, sums, line, gl,
):
    half = hat.shape[1]
    part_width = gc.shape[1]
    fill_taps(taps, spread_taps, True, part_width, part_width)
    sums[...] = jnp.zeros(sums.shape, F32)
    io.wait(0, 3)
    line[...] = hat[:, part_width:].astype(F32) * g_gain[:, part_width:] + g_shifts[0:1, part_width:]
    fill_shifts(lambda lanes: gc[:, lanes], moved, part_width)

    conv_rows(moved, spread_taps, low, high, 0, part_width, gl, line, sums)
    tap_sums(sums, gtaps_o)
    io.wait(1, 2, 4, 10, 11, 12)
    value = jnp.concatenate([gl_first[...], gl[...]], axis=1)
    hat32 = hat[...].astype(F32)
    gggain_o[...] = rows_sum(value * hat32)
    ggshift_o[...] = rows_sum(value)
    gz = normalize_back(value * g_gain[...], hat32, inv[:, 0:1])
    part = (gz * slope[:, half:].astype(F32)).astype(BF16)
    gh[...] = part
    gbin_o[...] = rows_sum(part.astype(F32))
    io.ship(1)
    g_nm = dot_nt(gh_first[:, :half], w_in[:, :half]) + dot_nt(gh[...], w_in[:, half:])
    u = y1[...].astype(BF16).astype(F32)
    uhat, uinv = normalize(u)
    ggain_o[...] = rows_sum(g_nm * uhat)
    gshift_o[...] = rows_sum(g_nm)
    gu_o[...] = normalize_back(g_nm * gain[...], uhat, uinv)


def gate_weights_kernel(exact, io, gh_first, gh, nm, keep, send, dw):
    half = gh.shape[1]
    for part, value in enumerate((gh_first, gh)):
        for k in range(half // 512):
            cols = slice(k * 512, (k + 1) * 512)
            dw[pl.ds(part * half + 512 * k, 512), :] = dot_tn(value[:, cols], nm[...]).astype(BF16)
    emit(
        place(exact), keep, send, 96, lambda start, count, part: dw[pl.ds(start, count), :],
        192, [(0, 0, 96, 0, 0), (0, 96, 96, 1, 0)],
    )


def attend_back_kernel(
    exact, io, y1, gatt, table, na, qu, qv, k, v, probs, ctx, w4, wo, gain, g2, e, gmix, zr, c,
    gu_o, keep, send, ggain_o, gvec_o,
    pk, gq, gk_turned, gv_turned, gpk_turned, gctx, dw,
):
    count = y1.shape[0]
    io.wait(1, 9)
    ga = gatt[...]
    gvec_o[5:6, :] = rows_sum(ga.astype(F32))
    dw[4] = dot_tn(ga, ctx[...]).astype(BF16)
    io.wait(11)
    gctx[...] = dot_nt(ga, wo[...]).astype(BF16)
    io.wait(2, 10)
    pk[...] = dot_nn(table[...], w4[3]).astype(BF16)
    io.wait(3, 4, 5, 6, 7, 8)
    row = lax.broadcasted_iota(jnp.int32, (count, count), 0)
    col = lax.broadcasted_iota(jnp.int32, (count, count), 1)
    mirror = jnp.where(row + col == count - 1, 1.0, 0.0).astype(BF16)
    zero = jnp.zeros((), BF16)
    scale = 1.0 / math.sqrt(512 // HEADS)
    first = head_mask(0, count)
    for pair in range(HEADS // 2):
        cols = slice(pair * 128, (pair + 1) * 128)
        gctx_turned, qu_turned, qv_turned = gctx[:, cols].T, qu[:, cols].T, qv[:, cols].T
        gqu, gqv = [], []
        for h in range(2):
            own = slice(64 * h, 64 * h + 64)
            rows = slice(pair * 128 + 64 * h, pair * 128 + 64 * h + 64)
            pr = probs[2 * pair + h]
            gc = jnp.where(head_mask(h, count), gctx[:, cols], zero)
            gprobs = dot_nt(gc, v[:, cols])
            gv_turned[rows, :] = dot_nn(gctx_turned[own], pr).astype(BF16)
            weighted = pr.astype(F32) * gprobs
            gs = weighted - pr.astype(F32) * jnp.sum(weighted, axis=1, keepdims=True)
            gs = gs.astype(BF16)
            gqu.append(dot_nn(gs, k[:, cols]))
            gk_turned[rows, :] = (dot_nn(qu_turned[own], gs) * scale).astype(BF16)
            turned = dot_nn(gs, mirror)
            wide = jnp.concatenate([turned, jnp.zeros((count, count), F32)], axis=1)
            wide = pltpu.roll(wide, 0, 1, stride=1, stride_axis=0).astype(BF16)
            gqv.append(dot_nn(wide, pk[:, cols]))
            gpk_turned[rows, :] = (dot_nn(qv_turned[own], wide) * scale).astype(BF16)
        a = jnp.where(first, gqu[0], gqu[1]) * scale
        b = jnp.where(first, gqv[0], gqv[1]) * scale
        gvec_o[3:4, cols] = rows_sum(a)
        gvec_o[4:5, cols] = rows_sum(b)
        gq[:, cols] = (a + b).astype(BF16)
    gk, gv = gk_turned[...].T, gv_turned[...].T
    gvec_o[1:2, :] = rows_sum(gq[...].astype(F32))
    gvec_o[2:3, :] = rows_sum(gv.astype(F32))
    dw[0] = dot_tn(gq[...], na[...]).astype(BF16)
    dw[1] = dot_nn(gk_turned[...], na[...]).astype(BF16)
    dw[2] = dot_nn(gv_turned[...], na[...]).astype(BF16)
    dw[3] = dot_nn(gpk_turned[...], table[...]).astype(BF16)
    io.wait(0, 12, 13, 14, 15, 16, 17)
    gg = g2[...].astype(BF16).T
    gm = gmix[...].T
    for part in range(2):
        dw[5 + part] = dot_nn(gg, e[:, part * 512 : (part + 1) * 512]).astype(BF16)
    for part in range(3):
        cols = slice(part * 512, (part + 1) * 512)
        gated = (zr[:, cols].astype(F32) * c[:, cols].astype(F32)).astype(BF16)
        dw[7 + part] = dot_nn(gm, gated).astype(BF16)
    emit(
        place(exact), keep, send, 160, lambda start, count, part: dw[part, pl.ds(start, count), :],
        32, [(part, 0, 32, part // 5, part % 5 * 32) for part in range(10)],
    )
    io.ship(1, 2)
    total = dot_nt(gq[...], w4[0]) + dot_nt(gk, w4[1]) + dot_nt(gv, w4[2])
    u = y1[...].astype(BF16).astype(F32)
    hat, inv = normalize(u)
    ggain_o[...] = rows_sum(total * hat)
    gvec_o[0:1, :] = rows_sum(total)
    gu_o[...] = normalize_back(total * gain[...], hat, inv)


def lane_piece(source, start, count):
    block, away = start // 128 * 128, start % 128
    wide = 128 if away + count <= 128 else 256
    value = source[:, block : block + wide]
    if away:
        value = pltpu.roll(value, wide - away, 1)
    return value


def pack_small(put, v512, v1024, v1536, v_rest, b1, b_in, packed):
    lane = lax.broadcasted_iota(jnp.int32, (32, 128), 1)
    row = lax.broadcasted_iota(jnp.int32, (32, 128), 0)
    for which in range(16):
        first = lane_piece(v512, 32 * which, 32)
        second = pltpu.roll(lane_piece(v1024, 64 * which, 64), 32, 1)
        third = lane_piece(v1536, 96 * which, 96)[:, :128]
        rest = lane_piece(v_rest, 96 * which, 96)[:, :128]
        bias = lane_piece(b_in, 192 * which, 192)
        rows = pl.ds(32 * which, 32)
        packed[rows, 0:128] = jnp.where(lane < 32, first, second).astype(BF16)
        packed[rows, 128:256] = third.astype(BF16)
        packed[rows, 256:384] = jnp.where(row < 8, rest, bias[:, :128]).astype(BF16)
        packed[rows, 384:512] = jnp.where(row < 8, b1[:, 128 * which : 128 * (which + 1)], bias[:, 128:]).astype(BF16)
    put(
        lambda start, count, part: packed[pl.ds(start, count), :],
        32, [(0, 0, 16, 0, 128), (0, 16, 16, 1, 128)],
    )


def last_kernel(
    exact, io, frames, p_in, g2, gu_a, gu_m, w1, w2, gains, shifts,
    gb1_r, ggain_r, gshift_r, gtaps_r, gmshift, gagain, gavec, gbin_0, gbin_1, gmgain, gmshift_0, gmshift_1,
    gggain, ggshift_0, ggshift_1, ggtaps_0, ggtaps_1,
    gx_o, keep, send, a, dw, v512, v1024, v1536, v_rest, b1, b_in, packed, hidden_sum,
):
    put = functools.partial(emit, place(exact), keep, send, 144)
    io.wait(0, 7, 8)
    x = frames[...].astype(F32)
    hat, inv = normalize(x)
    n = (hat * gains[0:1, :] + shifts[0:1, :]).astype(BF16)
    io.wait(1)
    for c in range(a.shape[1] // 512):
        cols = slice(c * 512, (c + 1) * 512)
        h = p_in[:, cols]
        a[:, cols] = (h * sigmoid(h)).astype(BF16)
    io.wait(2, 3, 4)
    g1 = g2[...] + gu_a[...] + gu_m[...]
    gf = (0.5 * g1).astype(BF16)
    io.wait(5, 6)
    g_hid = hidden_back(put, n, gf, p_in, a, w1, w2, hidden_sum, dw)
    gx_o[...] = g1 + normalize_back(g_hid * gains[0:1, :], hat, inv)
    io.ship(0)

    for ref in (v512, v1024, v_rest, b1, b_in):
        ref[...] = jnp.zeros(ref.shape, F32)
    io.wait(*range(9, 26))
    v512[0:1, :] = rows_sum(g_hid * hat)
    v512[1:3, :] = ggain_r[...]
    v512[3:4, :] = rows_sum(g_hid)
    v512[4:5, :] = rows_sum(gf.astype(F32))
    v512[5:9, :] = gshift_r[...]
    v512[9:10, :] = gagain[...]
    v512[10:16, :] = gavec[...]
    v512[16:17, :] = gmgain[...]
    v512[17:18, :] = gmshift_0[...]
    v512[18:19, :] = gmshift_1[...]
    v1024[0:31, :] = gtaps_r[...]
    v1024[31:32, :] = gmshift[...]
    part_width = ggtaps_0.shape[1]
    v1536[0:31, :part_width] = ggtaps_0[...]
    v1536[0:31, part_width:] = ggtaps_1[...]
    v1536[31:32, :] = gggain[...]
    v_rest[0:1, :] = ggshift_0[...]
    v_rest[1:2, :] = ggshift_1[...]
    b1[0:1, :] = hidden_sum[...]
    b1[1:2, :] = gb1_r[...]
    half = gbin_0.shape[1]
    b_in[8:9, :half] = gbin_0[...]
    b_in[8:9, half:] = gbin_1[...]
    pack_small(put, v512, v1024, v1536, v_rest, b1, b_in, packed)
    io.ship(1, 2)


def add_core_x(rows, io, keep, got, stay, away):
    add_rows(away, 0, 8 * rows, (keep, 8 * rows), (got, 8 * rows))
    io.ship(1)
    add_rows(stay, 0, 8 * rows, (keep, 0), (got, 0))


def add_middle(rows_a, rows_r, io, keep_a, got_a, stay_r, got_r, a_stay, a_away, r_stay, r_away):
    io.wait(0, 1)
    add_rows(a_away, 0, 8 * rows_a, (keep_a, 8 * rows_a), (got_a, 8 * rows_a))
    io.ship(1)
    io.wait(2, 3)
    add_rows(r_away, 0, 4 * rows_r, (stay_r, 4 * rows_r), (got_r, 4 * rows_r))
    io.ship(3)
    add_rows(a_stay, 0, 8 * rows_a, (keep_a, 0), (got_a, 0))
    io.ship(0)
    add_rows(r_stay, 0, 4 * rows_r, (stay_r, 0), (got_r, 0))


def tail_a_kernel(rows_f, io, keep_f, got_f, f_0, f_1, f_2, f_3):
    for at, ref in ((2, f_2), (1, f_1), (3, f_3), (0, f_0)):
        add_rows(ref, 0, 4 * rows_f, (keep_f, at * 4 * rows_f), (got_f, at * 4 * rows_f))
        io.ship(at)


def tail_b_kernel(rows_m, rows_a, rows_r, io, keep_m, got_m, stay_a, got_a, stay_r, got_r, m_0, m_1, m_2, m_3, stay, away):
    rows_z = 2 * rows_a + rows_r
    io.wait(2, 3, 4, 5)
    for odd, ref in ((1, away), (0, stay)):
        for high in range(2):
            at = 2 * high + odd
            for y in range(2):
                first = (y * 4 + at) * rows_a
                add_rows(ref, high * rows_z + y * rows_a, rows_a, (stay_a, first), (got_a, first))
            add_rows(ref, high * rows_z + 2 * rows_a, rows_r, (stay_r, at * rows_r), (got_r, at * rows_r))
        io.ship(4 + odd)
    io.wait(0, 1)
    for at, ref in ((2, m_2), (1, m_1), (3, m_3), (0, m_0)):
        add_rows(ref, 0, 4 * rows_m, (keep_m, at * 4 * rows_m), (got_m, at * 4 * rows_m))
        io.ship(at)


def tail_c_kernel(rows_f, rows_a, rows_r, io, f_0, f_1, f_2, f_3, stay, got, f_stay, f_away, z_stay, z_away):
    for odd, ref in ((1, f_away), (0, f_stay)):
        for high in range(2):
            first = (2 * high + odd) * rows_f
            add_rows(ref, high * rows_f, rows_f, *[(term, first) for term in (f_0, f_1, f_2, f_3)])
        io.ship(odd)
    rows_z = 2 * rows_a + rows_r
    for high, ref in ((1, z_away), (0, z_stay)):
        add_rows(ref, 0, rows_z, (stay, high * rows_z), (got, high * rows_z))
        io.ship(2 + high)


def tail_d_kernel(
    rows_m, rows_f, rows_a, rows_r, io, m_0, m_1, m_2, m_3, f_stay, f_got, z_stay, z_got,
    z_0, z_1, z_2, z_3, f_0, f_1, a_0, a_1, r_own,
):
    for at, ref in ((1, z_1), (2, z_2), (3, z_3), (0, z_0)):
        add_rows(ref, 0, rows_m, *[(term, at * rows_m) for term in (m_0, m_1, m_2, m_3)])
        io.ship(at)
    for high, ref in ((1, f_1), (0, f_0)):
        add_rows(ref, 0, rows_f, (f_stay, high * rows_f), (f_got, high * rows_f))
        io.ship(4 + high)
    for y, ref in ((1, a_1), (0, a_0)):
        add_rows(ref, 0, rows_a, (z_stay, y * rows_a), (z_got, y * rows_a))
        io.ship(6 + y)
    add_rows(r_own, 0, rows_r, (z_stay, 2 * rows_a), (z_got, 2 * rows_a))


def tail_e_kernel(rows_m, rows_f, rows_a, rows_r, io, m_0, m_1, m_2, m_3, f_0, f_1, a_0, a_1, r_own, out):
    add_rows(out, 0, rows_r, (r_own, 0))
    add_rows(out, rows_r, rows_m, (m_0, 0), (m_1, 0), (m_2, 0), (m_3, 0))
    add_rows(out, rows_r + rows_m, rows_a, (a_0, 0), (a_1, 0))
    add_rows(out, rows_r + rows_m + rows_a, rows_f, (f_0, 0), (f_1, 0))


def finish_kernel(
    io, side, own, far,
    ffn_in_o, b1_o, ffn_out_o, gains_o, shifts_o, m_taps_o, m_shift_o, merge_o, attn_o, attn_out_o, a_gain_o, a_vec_o,
    mlp_in_o, b_in_o, mlp_out_o, m_gain_o, m_shifts_o, g_gain_o, g_shifts_o, g_taps_o, small,
):
    def half(which, first, count, cols=slice(0, 512)):
        rows = slice(first, first + count)
        return jnp.where(side[0] == which, own[rows, cols], far[rows, cols]).astype(F32)

    def span(start, count):
        return slice(start, start + count)

    for q in range(4):
        cols = span(128 * q, 128)
        ffn_in_o[0, cols, :] = half(0, 384, 128, cols)
        ffn_in_o[1, cols, :] = half(0, 0, 128, cols)
        ffn_out_o[0, :, span(512 * q, 512)] = half(1, 384 + 32 * q, 32)
        ffn_out_o[1, :, span(512 * q, 512)] = half(1, 32 * q, 32)
    io.ship(0, 2)
    for part in range(2):
        mlp_in_o[span(96 * part, 96), :] = half(part, 128, 96)
        merge_o[:, span(512 * part, 512)] = half(1, 224 + 32 * part, 32)
        small[span(16 * part, 16), :] = half(part, 512, 16)
    for q in range(4):
        attn_o[q] = half(0, 224 + 32 * q, 32)
    attn_out_o[...] = half(0, 352, 32)
    for part in range(3):
        mlp_out_o[:, span(512 * part, 512)] = half(1, 288 + 32 * part, 32)
    io.ship(7, 8, 9, 12, 14)
    first = small[:, 0:128]
    gains_o[...] = first[0:3, 0:32]
    shifts_o[...] = first[3:9, 0:32]
    a_gain_o[...] = first[9:10, 0:32].reshape(32)
    a_vec_o[...] = first[10:16, 0:32]
    m_gain_o[...] = first[16:17, 0:32].reshape(32)
    m_shifts_o[...] = first[17:19, 0:32]
    second = pltpu.roll(first, 96, 1)
    m_taps_o[...] = second[0:31, 0:64]
    m_shift_o[...] = second[31:32, 0:64].reshape(64)
    third = small[:, 128:256]
    g_taps_o[...] = third[0:31, 0:96]
    g_gain_o[...] = third[31:32, 0:96].reshape(96)
    g_shifts_o[...] = small[0:2, 256:352]
    b_in_o[...] = small[8:9, 256:448].reshape(192)
    b1_o[...] = small[0:2, 384:512]


ANY = pl.BlockSpec(memory_space=pl.ANY)


def shape(dims, kind=F32):
    return jax.ShapeDtypeStruct(dims, kind)


class Kernel:
    def __init__(self, copies_in, copies_out):
        self.copies_in, self.copies_out, self.shipped = copies_in, copies_out, set()

    def wait(self, *which):
        for at in which:
            for copy in self.copies_in[at]:
                copy.wait()

    def ship(self, *which):
        for at in which:
            self.shipped.add(at)
            for copy in self.copies_out[at]:
                copy.start()


def run(body, args, outs, scratch=(), late=(), smem=(), after=(), mib=63):
    arrays, reads, holds = [], [], []
    for at, arg in enumerate(args):
        if isinstance(arg, tuple):
            array, layer = arg
            reads.append([(len(arrays), layer, None)])
            arrays.append(array)
            dims, kind = array.shape[1:], array.dtype
        else:
            pieces = arg if isinstance(arg, list) else [arg]
            rows = sum(piece.shape[0] for piece in pieces)
            first, read = 0, []
            for piece in pieces:
                read.append((len(arrays), None, (first, piece.shape[0]) if len(pieces) > 1 else None))
                arrays.append(piece)
                first += piece.shape[0]
            reads.append(read)
            dims, kind = (rows,) + pieces[0].shape[1:], pieces[0].dtype
        holds.append((pltpu.SMEM if at in smem else pltpu.VMEM)(dims, kind))
    shapes, writes = [], []
    for out in outs:
        pieces = out if isinstance(out, list) else [out]
        first, write = 0, []
        for piece in pieces:
            write.append((len(shapes), (first, piece.shape[0]) if len(pieces) > 1 else None))
            shapes.append(piece)
            first += piece.shape[0]
        writes.append(write)
        dims = (first,) + pieces[0].shape[1:] if isinstance(out, list) else out.shape
        holds.append(pltpu.VMEM(dims, pieces[0].dtype))
    n_in, n_after, n_out, n_args = len(arrays), len(after), len(shapes), len(args)

    def kernel(*refs):
        sources, refs = refs[:n_in], refs[n_in + n_after :]
        targets, refs = refs[:n_out], refs[n_out:]
        held, refs = refs[: len(holds)], refs[len(holds) :]
        in_sems, out_sems, refs = refs[0], refs[1], refs[2:]

        def rows_of(ref, span):
            return ref if span is None else ref.at[pl.ds(*span)]

        copies_in = [
            [
                pltpu.make_async_copy(
                    sources[source] if layer is None else sources[source].at[layer], rows_of(held[at], span),
                    in_sems.at[source],
                )
                for source, layer, span in read
            ]
            for at, read in enumerate(reads)
        ]
        copies_out = [
            [
                pltpu.make_async_copy(rows_of(held[n_args + at], span), targets[target], out_sems.at[target])
                for target, span in write
            ]
            for at, write in enumerate(writes)
        ]
        early = [at for at in range(n_args) if at not in late]
        for at in early + list(late):
            for copy in copies_in[at]:
                copy.start()
        state = Kernel(copies_in, copies_out)
        state.wait(*early)
        body(state, *held, *refs)
        state.ship(*[at for at in range(len(outs)) if at not in state.shipped])
        for copies in copies_out:
            for copy in copies:
                copy.wait()

    return pl.pallas_call(
        kernel,
        out_shape=tuple(shapes),
        in_specs=[ANY] * (n_in + n_after),
        out_specs=(ANY,) * n_out,
        scratch_shapes=holds
        + [pltpu.SemaphoreType.DMA((n_in,)), pltpu.SemaphoreType.DMA((n_out,))]
        + list(scratch),
        compiler_params=pltpu.CompilerParams(vmem_limit_bytes=mib * MIB),
        cost_estimate=pl.CostEstimate(flops=1, bytes_accessed=1, transcendentals=0),
    )(*arrays, *after)


def swap(value, x=0, y=0, z=0, core=0):
    away = 16 * x + 4 * z + 2 * y + core
    return lax.ppermute(value, ("branch", "dp"), [(source, source ^ away) for source in range(32)])


def across_xy(parts):
    return [swap(parts[1], y=1), swap(parts[2], x=1), swap(parts[3], x=1, y=1)]


def across_z(parts):
    return [swap(parts[at], z=at) for at in (1, 2, 3)]


def local(frames, lengths, cotangent, *weights):
    (
        ffn_in, ffn_in_bias, ffn_out, shared_gains, shared_shifts, merge_kernel, merge_shift, merge_weight,
        attn_weights, attn_out, attn_gain, attn_vectors, mlp_in, mlp_in_bias, mlp_out, mlp_gain, mlp_shifts,
        gate_gain, gate_shifts, gate_kernel,
    ) = weights
    size = lax.axis_size("dp")
    exact = size == 16 and lax.axis_size("branch") == 2
    count, width = frames.shape
    hidden = ffn_in.shape[2]
    half = gate_gain.shape[0]
    taps = gate_kernel.shape[0]
    down, up = tables(count, width)
    act = lambda cols, kind=F32: shape((count, cols), kind)
    vmem = lambda dims, kind=BF16: pltpu.VMEM(dims, kind)
    line = lambda rows, cols: shape((rows, cols))
    rows16 = lambda rows: shape((rows, 512), BF16)
    cut = lambda *rows: [rows16(piece) for piece in rows]
    rows_r, rows_a, rows_m, rows_f = 128, 160, 96, 144

    (
        y1, p1, low, high, na, qu, qv, k, v, probs, ctx, nm, slope, zr, c, hat, inv, activations, g2, e, joined, keep_r, send_r,
        gb1_r, ggain_r, gshift_r, attn_gain, mlp_gain, gate_gain,
    ) = run(
        functools.partial(forward_kernel, exact),
        (
            frames, lengths, cotangent, (ffn_in, 0), (ffn_in, 1), ffn_in_bias, (ffn_out, 0), (ffn_out, 1), shared_gains,
            shared_shifts, merge_kernel, merge_shift, merge_weight, attn_weights, attn_out, attn_gain, attn_vectors, mlp_in,
            mlp_in_bias, mlp_out, mlp_gain, mlp_shifts, gate_gain, gate_shifts, gate_kernel, down,
        ),
        (
            act(width), act(hidden), act(128, jnp.int32), act(128, jnp.int32), *(act(width, BF16),) * 5,
            shape((HEADS, count, count), BF16), act(width, BF16), act(width, BF16), act(2 * half, BF16), act(half, BF16),
            act(half, BF16), act(half, BF16), act(128), act(width, BF16), act(width), act(2 * width, BF16), act(2 * width),
            rows16(16 * rows_r), rows16(16 * rows_r), line(1, hidden), line(2, width), line(4, width),
            line(1, width), line(1, width), line(1, half),
        ),
        [
            vmem((count, width)), vmem((count, width)), vmem((2 * count, width)), vmem((count, count), F32),
            vmem((count, half)), vmem((count, half), F32), vmem((8, count + 32, half // 2), F32),
            vmem((taps, 8, half // 2), F32), vmem((count, hidden), F32), vmem((count, hidden)), vmem((512, hidden)),
            vmem((1, 2 * width), F32), vmem((1, 2 * half), F32),
        ],
        late=[FORWARD_IN.index(name) for name in FORWARD_LATER],
        smem=(1,),
    )
    got_r = swap(send_r, core=1) if exact else None
    gatt, gmix, gtaps_r, gmshift = run(
        merge_back_kernel,
        (g2, joined, merge_kernel, merge_weight, low, high),
        (act(width, BF16), act(width, BF16), line(taps, 2 * width), line(1, 2 * width)),
        [
            vmem((8, count + 32, 2 * width), F32), vmem((taps, 8, 2 * width), F32), vmem((taps, 8, 2 * width), F32),
            vmem((count, 2 * width), F32),
        ],
        late=(0, 3, 1, 4, 5),
    )
    if exact:
        stay_r, away_r = run(
            functools.partial(add_core_x, rows_r), (keep_r, got_r), (rows16(8 * rows_r),) * 2, after=[gatt]
        )
        got_r = swap(away_r, x=1)
    gu_a, keep_a, *send_a, gagain, gavec = run(
        functools.partial(attend_back_kernel, exact),
        (
            y1, gatt, up, na, qu, qv, k, v, probs, ctx, attn_weights, attn_out, attn_gain, g2, e, gmix, zr, c,
        ),
        (act(width), rows16(16 * rows_a), cut(864, 864, 832), line(1, width), line(6, width)),
        [
            vmem((2 * count, width)), vmem((count, width)), vmem((width, count)), vmem((width, count)),
            vmem((width, 2 * count)), vmem((count, width)), vmem((10, width, width)),
        ],
        late=(1, 9, 11, 2, 10, 8, 7, 6, 5, 4, 3, 13, 14, 15, 16, 17, 0, 12),
        after=[away_r] if exact else [],
    )
    got_a = [swap(piece, core=1) for piece in send_a] if exact else []
    part_width = half // 2
    conv_scratch = [
        vmem((8, count + 32, part_width), F32), vmem((taps, 8, part_width), F32), vmem((taps, 8, part_width), F32),
        vmem((count, part_width), F32),
    ]
    gh, gc, gl, gbin_0, ggshift_1, ggtaps_0, gmshift_1 = run(
        gate_back_first_kernel,
        (gmix, slope, zr, c, hat, mlp_out, gate_gain, gate_shifts, gate_kernel, low, high),
        (
            act(half, BF16), act(part_width), act(part_width), line(1, half), line(1, half), line(taps, part_width),
            line(1, width),
        ),
        conv_scratch,
        late=(0, 5, 3, 2, 1, 4),
        after=[gu_a],
    )
    if exact:
        stay_a, away_a, stay_r, away_r = run(
            functools.partial(add_middle, rows_a, rows_r),
            (keep_a, got_a, stay_r, got_r),
            (rows16(8 * rows_a), rows16(8 * rows_a), rows16(4 * rows_r), rows16(4 * rows_r)),
            late=(0, 1, 2, 3),
            after=[gh],
        )
        got_a, got_r = swap(away_a, x=1), swap(away_r, y=1)
    gu_m, gh_second, gbin_1, gggain, ggshift_0, ggtaps_1, gmgain, gmshift_0 = run(
        gate_back_second_kernel,
        (
            gc, gl, slope, hat, inv, gate_gain, gate_shifts, gate_kernel, low, high, y1, gh, mlp_in, mlp_gain,
        ),
        (
            act(width), act(half, BF16), line(1, half), line(1, half), line(1, half), line(taps, part_width),
            line(1, width), line(1, width),
        ),
        conv_scratch + [vmem((count, part_width), F32)],
        late=(0, 3, 1, 2, 4, 10, 11, 12),
        after=[away_a] if exact else [],
    )
    g_frames, keep_f, *send_f = run(
        functools.partial(last_kernel, exact),
        (
            frames, p1, g2, gu_a, gu_m, (ffn_in, 0), (ffn_out, 0), shared_gains, shared_shifts,
            gb1_r, ggain_r, gshift_r, gtaps_r, gmshift, gagain, gavec, gbin_0, gbin_1, gmgain, gmshift_0, gmshift_1,
            gggain, ggshift_0, ggshift_1, ggtaps_0, ggtaps_1,
        ),
        (act(width), rows16(16 * rows_f), cut(1152, 1152)),
        [
            vmem((count, hidden)), vmem((512, hidden)), vmem((32, width), F32),
            vmem((32, 2 * width), F32),
            vmem((32, half), F32), vmem((32, half), F32), vmem((32, hidden), F32), vmem((32, 2 * half), F32),
            vmem((512, 512)), vmem((1, hidden), F32),
        ],
        late=(0, 7, 8, 1, 2, 3, 4, 6, 5, *range(9, 26)),
        after=[got_r] if exact else [],
    )
    got_f = [swap(piece, core=1) for piece in send_f] if exact else []
    keep_m, *send_m = run(
        functools.partial(gate_weights_kernel, exact),
        (gh, gh_second, nm),
        (rows16(16 * rows_m), cut(768, 768)),
        [vmem((2 * half, 512))],
        after=[g_frames],
    )
    if exact:
        got_m = [swap(piece, core=1) for piece in send_m]
        sums = lambda *rows: tuple(rows16(count) for count in rows)
        small = functools.partial(run, mib=24)
        f = run(
            functools.partial(tail_a_kernel, rows_f), (keep_f, got_f), sums(*(4 * rows_f,) * 4), after=[keep_m]
        )
        f = (f[0], *across_xy(f))
        *m, z_stay, z_away, z_more = run(
            functools.partial(tail_b_kernel, rows_m, rows_a, rows_r),
            (keep_m, got_m, stay_a, got_a, stay_r, got_r),
            sums(*(4 * rows_m,) * 4, 4 * rows_a + 2 * rows_r) + (cut(2 * rows_a + rows_r, 2 * rows_a + rows_r),),
            late=(0, 1, 2, 3, 4, 5),
            after=[f[0]],
        )
        m = (m[0], *across_xy(m))
        f_stay, f_away, z_stay, z_away = small(
            functools.partial(tail_c_kernel, rows_f, rows_a, rows_r),
            (*f, z_stay, [swap(z_away, z=1), swap(z_more, z=1)]),
            sums(2 * rows_f, 2 * rows_f, *(2 * rows_a + rows_r,) * 2),
        )
        *m, f_stay, f_away, a_stay, a_away, r_own = small(
            functools.partial(tail_d_kernel, rows_m, rows_f, rows_a, rows_r),
            (*m, f_stay, swap(f_away, z=1), z_stay, swap(z_away, z=2)),
            sums(*(rows_m,) * 4, rows_f, rows_f, rows_a, rows_a, rows_r),
        )
        m = (m[0], *across_z(m))
        own, = small(
            functools.partial(tail_e_kernel, rows_m, rows_f, rows_a, rows_r),
            (*m, f_stay, swap(f_away, z=2), a_stay, swap(a_away, y=1), r_own),
            sums(rows_r + rows_f + rows_a + rows_m),
        )
        far = swap(own, x=1)
        side = lax.axis_index("branch").reshape(1).astype(jnp.int32)
        flat = lambda n: shape((n,))
        done = small(
            finish_kernel,
            (side, own, far),
            (
                shape((2, 512, 128)), line(2, 128), shape((2, 32, hidden)), line(3, 32), line(6, 32), line(taps, 64),
                flat(64), line(32, 2 * width), shape((4, 32, width)), line(32, width), flat(32), line(6, 32),
                line(192, width), flat(192), line(32, half), flat(32), line(2, 32), flat(96), line(2, 96),
                line(taps, 96),
            ),
            [vmem((32, 512), F32)],
            smem=(0,),
        )
        turned = {2, 7, 8, 9, 12, 14}
        done = [jnp.swapaxes(v, -1, -2) if at in turned else v for at, v in enumerate(done)]
    else:

        def scatter(value):
            part = lax.psum_scatter(value, "dp", scatter_dimension=0, tiled=True)
            return lax.psum(part, "branch").T

        def out_rows(rows):
            parts = rows.shape[1] // 32
            return rows.reshape(16, parts, 32, 512).transpose(0, 2, 1, 3).reshape(512, 512 * parts)

        def columns(rows):
            return rows.reshape(16, 128, 4, 128).transpose(0, 3, 2, 1).reshape(2048, 512)

        def pieces(rows, per):
            return rows[:, :, :per].transpose(1, 0, 2).reshape(rows.shape[1], 16 * per)

        def ordered(keep, send, rows):
            both = jnp.stack([keep.reshape(2, 2, 4, rows, 512), send.reshape(2, 2, 4, rows, 512)], axis=3)
            return both.astype(F32).transpose(2, 1, 3, 0, 4, 5).reshape(16, 2, rows, 512)

        r, a, m, f = [
            ordered(*group)
            for group in (
                (keep_r, send_r, rows_r), (keep_a, jnp.concatenate(send_a), rows_a),
                (keep_m, jnp.concatenate(send_m), rows_m), (keep_f, jnp.concatenate(send_f), rows_f),
            )
        ]
        small = jnp.concatenate([f[:, 0, 128:], f[:, 1, 128:]], axis=1)
        vectors = pieces(small[:, 0:19], 32)
        m_both, g_both = pieces(small[:, :, 32:], 64), pieces(small[:, :, 128:], 96)
        done = [
            jnp.stack([scatter(columns(v)) for v in (f[:, 0, :128], r[:, 0])]),
            pieces(small[:, 0:2, 384:], 128),
            jnp.stack([scatter(out_rows(v)) for v in (f[:, 1, :128], r[:, 1])]),
            vectors[0:3], vectors[3:9], m_both[:31], m_both[31],
            scatter(out_rows(a[:, 1, :64])),
            jnp.stack([scatter(out_rows(a[:, 0, 32 * i : 32 * i + 32])) for i in range(4)]),
            scatter(out_rows(a[:, 0, 128:])),
            vectors[9], vectors[10:16],
            scatter(m.reshape(3072, 512)),
            pieces(small[:, 8:9, 256:], 192)[0],
            scatter(out_rows(a[:, 1, 64:])),
            vectors[16], vectors[17:19], g_both[31], pieces(small[:, 0:2, 256:], 96), g_both[:31],
        ]
        for at, v in enumerate(done):
            if at not in (0, 2, 7, 8, 9, 12, 14):
                part = lax.psum_scatter(v, "dp", scatter_dimension=v.ndim - 1, tiled=True)
                done[at] = lax.psum(part, "branch")
    return (activations, g_frames) + tuple(done)


def solution(mesh):
    rows = P(("branch", "dp"), None)
    last = {1: P("dp"), 2: P(None, "dp"), 3: P(None, None, "dp")}
    ranks = (3, 2, 3, 2, 2, 2, 1, 2, 3, 2, 1, 2, 2, 1, 2, 1, 2, 1, 2, 2)
    return jax.shard_map(
        local,
        mesh=mesh,
        in_specs=(rows,) * 3 + (P(),) * 20,
        out_specs=(rows, rows) + tuple(last[r] for r in ranks),
        check_vma=False,
    )
```

```python
import functools
import math

import jax
import jax.numpy as jnp
import numpy as np
from jax import lax
from jax.experimental import pallas as pl
from jax.experimental.pallas import tpu as pltpu
from jax.sharding import PartitionSpec as P

HEADS = 8
EPS = 1e-05
F32 = jnp.float32
BF16 = jnp.bfloat16
MIB = 1024 * 1024


def dot_nn(a, b):
    return lax.dot_general(a, b, (((1,), (0,)), ((), ())), preferred_element_type=F32)


def dot_nt(a, b):
    return lax.dot_general(a, b, (((1,), (1,)), ((), ())), preferred_element_type=F32)


def dot_tn(a, b):
    return lax.dot_general(a, b, (((0,), (0,)), ((), ())), preferred_element_type=F32)


def sigmoid(v):
    return 0.5 * jnp.tanh(0.5 * v) + 0.5


def normalize(v):
    center = v - jnp.mean(v, axis=-1, keepdims=True)
    spread = jnp.mean(center * center, axis=-1, keepdims=True)
    inverse = lax.rsqrt(spread + EPS)
    return center * inverse, inverse


def normalize_back(g_hat, hat, inverse):
    return inverse * (
        g_hat
        - jnp.mean(g_hat, axis=-1, keepdims=True)
        - hat * jnp.mean(g_hat * hat, axis=-1, keepdims=True)
    )


def rows_sum(v):
    return jnp.sum(v, axis=0, keepdims=True)


def tables(frame_count, width):
    distance = np.arange(frame_count - 1, -frame_count, -1).astype(np.float32)
    rates = np.exp(np.arange(0, width, 2).astype(np.float32) * np.float32(-math.log(10000.0) / width))
    angles = (distance[:, None] * rates[None, :].astype(np.float32)).astype(np.float64)
    rows = np.stack([np.sin(angles), np.cos(angles)], axis=-1).reshape(2 * frame_count - 1, width)
    zero = np.zeros((1, width))
    down = np.concatenate([rows, zero], axis=0).astype(np.float32)
    up = np.concatenate([rows[::-1], zero], axis=0).astype(np.float32)
    return jnp.asarray(down, BF16), jnp.asarray(up, BF16)


def fill_shifts(values_of, shifts_ref, width):
    rows = shifts_ref.shape[1]
    count = rows - 32

    def each(c, carry):
        lanes = pl.ds(pl.multiple_of(c * 128, 128), 128)
        shifts_ref[0, pl.ds(0, 16), lanes] = jnp.zeros((16, 128), F32)
        shifts_ref[0, pl.ds(16, count), lanes] = values_of(lanes)
        shifts_ref[0, pl.ds(16 + count, 16), lanes] = jnp.zeros((16, 128), F32)
        whole = shifts_ref[0, :, lanes]
        for s in range(1, 8):
            shifts_ref[s, :, lanes] = pltpu.roll(whole, rows - s, 0)
        return carry

    lax.fori_loop(0, width // 128, each, 0)


def fill_taps(kernel_ref, taps_ref, reverse, first_lane, width):
    taps = kernel_ref.shape[0]
    for t in range(taps):
        source = taps - 1 - t if reverse else t
        row = kernel_ref[pl.ds(source, 1), first_lane : first_lane + width]
        taps_ref[t, :, 0:width] = jnp.broadcast_to(row, (8, width))


def conv_rows(
    shifts_ref, taps_ref, low_ref, high_ref, first_lane, width, target_ref, values_ref=None, sums_ref=None, accumulate=False
):
    taps = taps_ref.shape[0]
    reach = taps // 2
    count = shifts_ref.shape[1] - 32
    row_tiles, lane_tiles = 4, 2
    row_blocks = count // (8 * row_tiles)

    def each(step, carry):
        block = step % row_blocks
        lane0 = pl.multiple_of((step // row_blocks) * (128 * lane_tiles), 128 * lane_tiles)
        row0 = pl.multiple_of(block * (8 * row_tiles), 8 * row_tiles)
        here = pl.ds(row0, 8 * row_tiles)
        near_lanes = pl.ds(lane0, 128 * lane_tiles)
        far_lanes = pl.ds(lane0 + first_lane, 128 * lane_tiles)
        shifts_here = shifts_ref.at[:, pl.ds(row0, 8 * row_tiles + 32), near_lanes]
        taps_here = taps_ref.at[:, :, near_lanes]
        low_here, high_here = low_ref.at[here, :], high_ref.at[here, :]
        rows = [pl.ds(8 * r, 8) for r in range(row_tiles)]
        lanes = [pl.ds(128 * l, 128) for l in range(lane_tiles)]
        low = [low_here[rows[r], :] for r in range(row_tiles)]
        high = [high_here[rows[r], :] for r in range(row_tiles)]
        total = [[None] * lane_tiles for r in range(row_tiles)]
        held = None
        if values_ref is not None:
            values_here = values_ref.at[here, far_lanes]
            sums_here = sums_ref.at[:, :, near_lanes]
            held = [[values_here[rows[r], lanes[l]] for l in range(lane_tiles)] for r in range(row_tiles)]
        for t in range(taps):
            away = t - reach
            start = 16 + away
            turn, base = start % 8, (start // 8) * 8
            tap = [taps_here[t, :, lanes[l]] for l in range(lane_tiles)]
            added = [None] * lane_tiles
            for r in range(row_tiles):
                same = None
                if away < 0:
                    same = low[r] <= away
                elif away > 0:
                    same = high[r] > away
                for l in range(lane_tiles):
                    near = shifts_here[turn, pl.ds(base + 8 * r, 8), lanes[l]]
                    if same is not None:
                        near = jnp.where(same, near, 0.0)
                    term = near * tap[l]
                    total[r][l] = term if total[r][l] is None else total[r][l] + term
                    if held is not None:
                        cross = near * held[r][l]
                        added[l] = cross if added[l] is None else added[l] + cross
            if held is not None:
                for l in range(lane_tiles):
                    sums_here[t, :, lanes[l]] += added[l]
        target_here = target_ref.at[here, far_lanes]
        for r in range(row_tiles):
            for l in range(lane_tiles):
                value = total[r][l]
                if accumulate:
                    value = target_here[rows[r], lanes[l]] + value
                target_here[rows[r], lanes[l]] = value
        return carry

    lax.fori_loop(0, row_blocks * (width // (128 * lane_tiles)), each, 0, unroll=2)


def tap_sums(sums_ref, out_ref):
    taps = sums_ref.shape[0]
    for t in range(taps):
        out_ref[pl.ds(taps - 1 - t, 1), :] = rows_sum(sums_ref[t])


def place(exact):
    if not exact:
        return None
    dp = lax.axis_index("dp")
    return lax.axis_index("branch"), (dp >> 2) & 3, (dp >> 1) & 1, dp & 1


def emit(here, keep, send, rows, value_of, per, parts):
    for group in range(8):
        z, y = group // 2, group % 2
        for side, ref in ((0, keep), (1, send)):
            for part, first, count, half, row in parts:
                if here is None:
                    base = ((half * 2 + y) * 4 + z) * rows + row
                    begin = (2 * group + side) * per + first
                else:
                    cx, cz, cy, core = here
                    base = pl.multiple_of((((half ^ cx) * 2 + (y ^ cy)) * 4 + (z ^ cz)) * rows + row, 16)
                    begin = pl.multiple_of((2 * group + (core ^ side)) * per + first, 16)
                ref[pl.ds(base, count), :] = value_of(begin, count, part)


def emit_whole(ref, rows, value_of, per, parts):
    for which in range(16):
        for part, first, count, row in parts:
            ref[pl.ds(which * rows + row, count), :] = value_of(which * per + first, count, part)


def add_rows(target, row, count, *terms):
    step = max(step for step in range(16, 257, 16) if count % step == 0)

    def each(at, carry):
        away = pl.multiple_of(at * step, 16)
        values = [ref[pl.ds(away + first, step), :] for ref, first in terms]
        if len(values) == 2:
            total = values[0] + values[1]
        else:
            total = functools.reduce(jnp.add, [value.astype(F32) for value in values]).astype(BF16)
        target[pl.ds(away + row, step), :] = total
        return carry

    lax.fori_loop(0, count // step, each, 0)


def front_part(io, frames, lengths, gains, shifts, b1, w1, w2, y1_o, p_o, low_o, high_o):
    count = frames.shape[0]
    x = frames[...].astype(F32)
    hat, _ = normalize(x)
    n = (hat * gains[0:1, :] + shifts[0:1, :]).astype(BF16)

    where = lax.broadcasted_iota(jnp.int32, (count, 128), 0)
    begin = jnp.zeros((count, 128), jnp.int32)
    end = jnp.full((count, 128), count, jnp.int32)
    bound = jnp.int32(0)
    for s in range(lengths.shape[1]):
        bound = bound + lengths[0, s]
        before = bound <= where
        begin = jnp.where(before, bound, begin)
        end = jnp.where(before, end, jnp.minimum(end, bound))
    low_o[...] = begin - where
    high_o[...] = end - where
    io.ship("low", "high")
    io.wait("w1_0", "w2_0")
    total = jnp.zeros(x.shape, F32)
    for c in range(w1.shape[1] // 512):
        cols = slice(c * 512, (c + 1) * 512)
        p = dot_nn(n, w1[:, cols]) + b1[0:1, cols]
        p_o[:, cols] = p
        a = (p * sigmoid(p)).astype(BF16)
        total = total + dot_nn(a, w2[cols, :])
    io.ship("p1")
    y1_o[...] = x + 0.5 * (total + shifts[1:2, :])
    io.ship("y1")


def head_mask(which, rows):
    lane = lax.broadcasted_iota(jnp.int32, (rows, 128), 1)
    return (lane < 64) if which == 0 else (lane >= 64)


def attend_part(
    io, y1, table, w4, wo, gain, vec, low, high,
    att_o, na_o, qu_o, qv_o, k_o, v_o, probs_o, ctx_o, pk, bias,
):
    count = y1.shape[0]
    u = y1[...].astype(BF16).astype(F32)
    hat, _ = normalize(u)
    na = (hat * gain[...] + vec[0:1, :]).astype(BF16)
    na_o[...] = na
    io.wait("w4", "table")
    q = dot_nn(na, w4[0]) + vec[1:2, :]
    qu_o[...] = (q + vec[3:4, :]).astype(BF16)
    qv_o[...] = (q + vec[4:5, :]).astype(BF16)
    k_o[...] = dot_nn(na, w4[1]).astype(BF16)
    v_o[...] = (dot_nn(na, w4[2]) + vec[2:3, :]).astype(BF16)
    pk[...] = dot_nn(table[...], w4[3]).astype(BF16)
    row = lax.broadcasted_iota(jnp.int32, (count, 128), 0)
    lane = lax.broadcasted_iota(jnp.int32, (count, 128), 1)
    for c in range(count // 128):
        away = lane + c * 128 - row
        same = (low[...] <= away) & (high[...] > away)
        bias[:, c * 128 : (c + 1) * 128] = jnp.where(same, 0.0, -1e30)
    io.ship("na", "qu", "qv", "k", "v")
    scale = 1.0 / math.sqrt(512 // HEADS)
    for pair in range(HEADS // 2):
        cols = slice(pair * 128, (pair + 1) * 128)
        outs = []
        for h in range(2):
            mask = head_mask(h, count)
            qu = jnp.where(mask, qu_o[:, cols], jnp.zeros((), BF16))
            qv = jnp.where(mask, qv_o[:, cols], jnp.zeros((), BF16))
            content = dot_nt(qu, k_o[:, cols])
            distant = dot_nt(qv, pk[:, cols])
            distant = pltpu.roll(distant, count + 1, 1, stride=1, stride_axis=0)[:, :count]
            scores = (content + distant) * scale + bias[...]
            weights = jnp.exp(scores - jnp.max(scores, axis=1, keepdims=True))
            probs = weights * (1.0 / jnp.sum(weights, axis=1, keepdims=True))
            probs = probs.astype(BF16)
            probs_o[2 * pair + h] = probs
            outs.append(dot_nn(probs, v_o[:, cols]))
        ctx_o[:, cols] = jnp.where(head_mask(0, count), outs[0], outs[1]).astype(BF16)
    io.ship("probs", "ctx")
    io.wait("wo")
    att_o[...] = (dot_nn(ctx_o[...], wo[...]) + vec[5:6, :]).astype(BF16)


def gate_part(
    io, y1, w_in, b_in, w_out, gain, shifts, g_gain, g_shifts, taps, low, high,
    mix_o, nm_o, slope_o, zr_o, c_o, hat_o, inv_o, gated, zg, moved, spread_taps,
):
    half = zr_o.shape[1]
    u = y1[...].astype(BF16).astype(F32)
    hat, _ = normalize(u)
    nm = (hat * gain[...] + shifts[0:1, :]).astype(BF16)
    nm_o[...] = nm
    io.wait("w_in")
    for c in range(w_in.shape[1] // 512):
        cols = slice(c * 512, (c + 1) * 512)
        h = dot_nn(nm, w_in[:, cols]) + b_in[:, cols]
        cdf = 0.5 + 0.5 * lax.erf(h * math.sqrt(0.5))
        z = h * cdf
        slope = cdf + h * (jnp.exp(-0.5 * h * h) * (1.0 / math.sqrt(2.0 * math.pi)))
        slope_o[:, cols] = slope.astype(BF16)
        if c < half // 512:
            zr_o[:, cols] = z.astype(BF16)
        else:
            zg[:, c * 512 - half : (c + 1) * 512 - half] = z
    io.ship("nm", "slope", "zr")
    v = zg[...]
    center = v - jnp.mean(v, axis=-1, keepdims=True)
    inverse = lax.rsqrt(jnp.mean(center * center, axis=-1, keepdims=True) + EPS)
    zg[...] = center * inverse
    inv_o[...] = jnp.broadcast_to(inverse, inv_o.shape)
    hat_o[...] = zg[...].astype(BF16)
    io.ship("hat", "inv")

    width = moved.shape[2]
    for first in range(0, half, width):

        def line(lanes, first=first):
            far = pl.ds(lanes.start + first, lanes.size)
            return zg[:, far] * g_gain[:, far] + g_shifts[0:1, far]

        fill_shifts(line, moved, width)
        fill_taps(taps, spread_taps, False, first, width)
        conv_rows(moved, spread_taps, low, high, first, width, zg)
    for c in range(half // 512):
        cols = slice(c * 512, (c + 1) * 512)
        mixed = zg[:, cols] + g_shifts[1:2, cols]
        c_o[:, cols] = mixed.astype(BF16)
        gated[:, cols] = (zr_o[:, cols].astype(F32) * mixed).astype(BF16)
    io.ship("c")
    io.wait("w_out")
    mix_o[...] = (dot_nn(gated[...], w_out[...]) + shifts[1:2, :]).astype(BF16)


def rear_part(
    io, y1, att, mix, cot, w1, b1, w2, gains, shifts, taps, m_shift, wm, low, high,
    act_o, g2_o, e, joined, out, gb1_o, ggain_o, gshift_o,
    moved, spread_taps, p, a, dw,
):
    width = joined.shape[1]
    joined[:, :512] = att[...].astype(F32)
    joined[:, 512:] = mix[...].astype(F32)
    io.ship("joined")

    for first in range(0, width, 512):
        fill_shifts(lambda lanes: joined[:, pl.ds(lanes.start + first, lanes.size)], moved, 512)
        fill_taps(taps, spread_taps, False, first, 512)
        conv_rows(moved, spread_taps, low, high, first, 512, p)
    e[...] = (joined[...] + p[:, :width] + m_shift[...]).astype(BF16)
    io.ship("e")
    io.wait("wm")
    y2 = y1[...] + dot_nn(e[...], wm[...]) + shifts[5:6, :]
    hat2, inv2 = normalize(y2)
    n = (hat2 * gains[1:2, :] + shifts[2:3, :]).astype(BF16)
    io.wait("w1_1", "w2_1", "cot")
    total = jnp.zeros(y2.shape, F32)
    for c in range(w1.shape[1] // 512):
        cols = slice(c * 512, (c + 1) * 512)
        h = dot_nn(n, w1[:, cols]) + b1[1:2, cols]
        p[:, cols] = h
        act = (h * sigmoid(h)).astype(BF16)
        a[:, cols] = act
        total = total + dot_nn(act, w2[cols, :])
    y3 = y2 + 0.5 * (total + shifts[3:4, :])
    hat3, inv3 = normalize(y3)
    act_o[...] = (hat3 * gains[2:3, :] + shifts[4:5, :]).astype(BF16)
    io.ship("act")

    g = cot[...].astype(F32)
    ggain_o[1:2, :] = rows_sum(g * hat3)
    gshift_o[2:3, :] = rows_sum(g)
    g3 = normalize_back(g * gains[2:3, :], hat3, inv3)
    gf = (0.5 * g3).astype(BF16)
    gshift_o[1:2, :] = rows_sum(gf.astype(F32))

    def put(value_of, per, parts):
        rows = [(part, first, count, half * 128 + row) for part, first, count, half, row in parts]
        emit_whole(out, 320, value_of, per, rows)

    g_hid = hidden_back(put, n, gf, p, a, w1, w2, gb1_o, dw)
    ggain_o[0:1, :] = rows_sum(g_hid * hat2)
    gshift_o[0:1, :] = rows_sum(g_hid)
    g2 = g3 + normalize_back(g_hid * gains[1:2, :], hat2, inv2)
    g2_o[...] = g2
    gg = g2.astype(BF16)
    turned = gg.T
    for part in range(2):
        cols = slice(part * 512, (part + 1) * 512)
        dw[:, cols] = dot_nn(turned, e[:, cols]).astype(BF16)
    emit_whole(
        out, 320, lambda start, count, part: dw[pl.ds(start, count), part * 512 : (part + 1) * 512],
        32, [(part, 0, 32, 256 + 32 * part) for part in range(2)],
    )
    io.ship("out_r")
    gshift_o[3:4, :] = rows_sum(gg.astype(F32))


FORWARD_IN = (
    "frames", "lengths", "cot", "w1_0", "w1_1", "b1", "w2_0", "w2_1", "gains", "shifts", "m_taps", "m_shift", "wm",
    "w4", "wo", "a_gain", "vec", "w_in", "b_in", "w_out", "m_gain", "m_shifts", "g_gain", "g_shifts", "g_taps",
    "table",
)
FORWARD_OUT = (
    "y1", "p1", "low", "high", "na", "qu", "qv", "k", "v", "probs", "ctx", "nm", "slope", "zr", "c", "hat", "inv",
    "act", "g2", "e", "joined", "out_r", "gb1", "ggain", "gshift", "a_gain_row", "m_gain_row",
    "g_gain_row",
)
FORWARD_LATER = (
    "w1_0", "w2_0", "a_gain", "vec", "m_shift", "b_in", "m_gain", "m_shifts", "g_gain", "g_shifts", "g_taps",
    "m_taps", "w4", "table", "wo", "w_in", "w_out", "wm", "cot", "w1_1", "w2_1",
)


class Named:
    def __init__(self, io):
        self.io = io

    def wait(self, *names):
        self.io.wait(*[FORWARD_IN.index(name) for name in names])

    def ship(self, *names):
        self.io.ship(*[FORWARD_OUT.index(name) for name in names])


def forward_kernel(io, *refs):
    i = dict(zip(FORWARD_IN, refs))
    o = dict(zip(FORWARD_OUT, refs[len(FORWARD_IN) :]))
    (
        att, mix, pk, bias, gated, zg, moved, spread_taps, p, a, dw, m_shift, b_in,
    ) = refs[len(FORWARD_IN) + len(FORWARD_OUT) :]
    io = Named(io)
    front_part(
        io, i["frames"], i["lengths"], i["gains"], i["shifts"], i["b1"], i["w1_0"], i["w2_0"],
        o["y1"], o["p1"], o["low"], o["high"],
    )
    io.wait("a_gain", "vec", "m_shift", "b_in", "m_gain", "m_shifts", "g_gain", "g_shifts", "g_taps", "m_taps")
    for source, target in (
        ("a_gain", o["a_gain_row"]), ("m_gain", o["m_gain_row"]), ("g_gain", o["g_gain_row"]), ("m_shift", m_shift),
        ("b_in", b_in),
    ):
        target[...] = i[source][...].reshape(target.shape)
    io.ship("a_gain_row", "m_gain_row", "g_gain_row")
    attend_part(
        io, o["y1"], i["table"], i["w4"], i["wo"], o["a_gain_row"], i["vec"], o["low"], o["high"],
        att, o["na"], o["qu"], o["qv"], o["k"], o["v"], o["probs"], o["ctx"], pk, bias,
    )
    gate_part(
        io, o["y1"], i["w_in"], b_in, i["w_out"], o["m_gain_row"], i["m_shifts"], o["g_gain_row"], i["g_shifts"],
        i["g_taps"], o["low"], o["high"],
        mix, o["nm"], o["slope"], o["zr"], o["c"], o["hat"], o["inv"], gated, zg, moved, spread_taps,
    )
    rear_part(
        io, o["y1"], att, mix, i["cot"], i["w1_1"], i["b1"], i["w2_1"], i["gains"], i["shifts"], i["m_taps"],
        m_shift, i["wm"], o["low"], o["high"],
        o["act"], o["g2"], o["e"], o["joined"], o["out_r"], o["gb1"], o["ggain"], o["gshift"],
        moved, spread_taps, p, a, dw,
    )


def merge_back_kernel(
    io, g2, joined, taps, wm, low, high, gatt_o, gmix_o, gtaps_o, gmshift_o, moved, spread_taps, sums, ge,
):
    width = joined.shape[1]
    fill_taps(taps, spread_taps, True, 0, width)
    sums[...] = jnp.zeros(sums.shape, F32)
    io.wait(0, 3)
    value = dot_nt(g2[...].astype(BF16), wm[...])
    gmshift_o[...] = rows_sum(value)
    ge[...] = value
    fill_shifts(lambda lanes: ge[:, lanes], moved, width)
    io.wait(1, 4, 5)

    conv_rows(moved, spread_taps, low, high, 0, width, ge, joined, sums, True)
    tap_sums(sums, gtaps_o)
    gatt_o[...] = ge[:, :512].astype(BF16)
    gmix_o[...] = ge[:, 512:].astype(BF16)


def hidden_back(put, n, gf, p, a, w1, w2, gb1_o, dw):
    hidden = p.shape[1]
    turned = gf.T
    for c in range(hidden // 512):
        cols = slice(c * 512, (c + 1) * 512)
        dw[:, cols] = dot_nn(turned, a[:, cols]).astype(BF16)
    put(
        lambda start, count, part: dw[pl.ds(start, count), part * 512 : (part + 1) * 512],
        32, [(part, 0, 32, 1, 32 * part) for part in range(hidden // 512)],
    )
    total = jnp.zeros(n.shape, F32)
    for c in range(hidden // 512):
        cols = slice(c * 512, (c + 1) * 512)
        h = p[:, cols]
        s = sigmoid(h)
        ga = dot_nt(gf, w2[cols, :])
        gp = (ga * (s * (1.0 + h * (1.0 - s)))).astype(BF16)
        gb1_o[:, cols] = rows_sum(gp.astype(F32))
        a[:, cols] = gp
        total = total + dot_nt(gp, w1[:, cols])
    turned = n.T
    for c in range(hidden // 512):
        cols = slice(c * 512, (c + 1) * 512)
        dw[:, cols] = dot_nn(turned, a[:, cols]).astype(BF16)

    def quarters(start, count, part):
        lanes = start if isinstance(start, int) else pl.multiple_of(start, 128)
        return jnp.concatenate([dw[pl.ds(128 * q, count), pl.ds(lanes, 128)] for q in range(4)], axis=1)

    put(quarters, 128, [(0, 0, 128, 0, 0)])
    return total


def gate_back_first_kernel(
    io, gmix, slope, zr, c, hat, w_out, g_gain, g_shifts, taps, low, high,
    gh, gc_o, gl_o, gbin_o, ggshift_o, gtaps_o, gmshift_o, moved, spread_taps, sums, line,
):
    half = zr.shape[1]
    part_width = line.shape[1]
    fill_taps(taps, spread_taps, True, 0, part_width)
    sums[...] = jnp.zeros(sums.shape, F32)
    io.wait(0, 1, 2, 3, 5)
    gm = gmix[...]
    gmshift_o[...] = rows_sum(gm.astype(F32))
    for k in range(half // 256):
        cols = slice(k * 256, (k + 1) * 256)
        gg = dot_nt(gm, w_out[cols, :]).astype(BF16).astype(F32)
        gzr = gg * c[:, cols].astype(F32)
        gc = gg * zr[:, cols].astype(F32)
        part = (gzr * slope[:, cols].astype(F32)).astype(BF16)
        gh[:, cols] = part
        gbin_o[:, cols] = rows_sum(part.astype(F32))
        ggshift_o[:, cols] = rows_sum(gc)
        if k * 256 < part_width:
            moved[0, pl.ds(16, 256), cols] = gc
        else:
            gc_o[:, k * 256 - part_width : (k + 1) * 256 - part_width] = gc
    io.ship(0, 1, 3, 4, 6)
    io.wait(4)
    line[...] = hat[:, :part_width].astype(F32) * g_gain[:, :part_width] + g_shifts[0:1, :part_width]
    fill_shifts(lambda lanes: moved[0, pl.ds(16, 256), lanes], moved, part_width)

    conv_rows(moved, spread_taps, low, high, 0, part_width, gl_o, line, sums)
    tap_sums(sums, gtaps_o)


def gate_back_second_kernel(
    io, gc, gl_first, slope, hat, inv, g_gain, g_shifts, taps, low, high, y1, gh_first, w_in, gain,
    gu_o, gh, gbin_o, gggain_o, ggshift_o, gtaps_o, ggain_o, gshift_o, moved, spread_taps, sums, line, gl,
):
    half = hat.shape[1]
    part_width = gc.shape[1]
    fill_taps(taps, spread_taps, True, part_width, part_width)
    sums[...] = jnp.zeros(sums.shape, F32)
    io.wait(0, 3)
    line[...] = hat[:, part_width:].astype(F32) * g_gain[:, part_width:] + g_shifts[0:1, part_width:]
    fill_shifts(lambda lanes: gc[:, lanes], moved, part_width)

    conv_rows(moved, spread_taps, low, high, 0, part_width, gl, line, sums)
    tap_sums(sums, gtaps_o)
    io.wait(1, 2, 4, 10, 11, 12)
    value = jnp.concatenate([gl_first[...], gl[...]], axis=1)
    hat32 = hat[...].astype(F32)
    gggain_o[...] = rows_sum(value * hat32)
    ggshift_o[...] = rows_sum(value)
    gz = normalize_back(value * g_gain[...], hat32, inv[:, 0:1])
    part = (gz * slope[:, half:].astype(F32)).astype(BF16)
    gh[...] = part
    gbin_o[...] = rows_sum(part.astype(F32))
    io.ship(1)
    g_nm = dot_nt(gh_first[:, :half], w_in[:, :half]) + dot_nt(gh[...], w_in[:, half:])
    u = y1[...].astype(BF16).astype(F32)
    uhat, uinv = normalize(u)
    ggain_o[...] = rows_sum(g_nm * uhat)
    gshift_o[...] = rows_sum(g_nm)
    gu_o[...] = normalize_back(g_nm * gain[...], uhat, uinv)


def gate_weights_kernel(exact, io, gh_first, gh, nm, keep, send, dw):
    half = gh.shape[1]
    for part, value in enumerate((gh_first, gh)):
        for k in range(half // 512):
            cols = slice(k * 512, (k + 1) * 512)
            dw[pl.ds(part * half + 512 * k, 512), :] = dot_tn(value[:, cols], nm[...]).astype(BF16)
    emit(
        place(exact), keep, send, 96, lambda start, count, part: dw[pl.ds(start, count), :],
        192, [(0, 0, 96, 0, 0), (0, 96, 96, 1, 0)],
    )


def attend_back_kernel(
    exact, io, y1, gatt, table, na, qu, qv, k, v, probs, ctx, w4, wo, gain, gmix, zr, c,
    gu_o, keep, send, ggain_o, gvec_o,
    pk, gq, gk_turned, gv_turned, gpk_turned, gctx, dw,
):
    count = y1.shape[0]
    io.wait(1, 9)
    ga = gatt[...]
    gvec_o[5:6, :] = rows_sum(ga.astype(F32))
    dw[4] = dot_tn(ga, ctx[...]).astype(BF16)
    io.wait(11)
    gctx[...] = dot_nt(ga, wo[...]).astype(BF16)
    io.wait(2, 10)
    pk[...] = dot_nn(table[...], w4[3]).astype(BF16)
    io.wait(3, 4, 5, 6, 7, 8)
    row = lax.broadcasted_iota(jnp.int32, (count, count), 0)
    col = lax.broadcasted_iota(jnp.int32, (count, count), 1)
    mirror = jnp.where(row + col == count - 1, 1.0, 0.0).astype(BF16)
    zero = jnp.zeros((), BF16)
    scale = 1.0 / math.sqrt(512 // HEADS)
    first = head_mask(0, count)
    for pair in range(HEADS // 2):
        cols = slice(pair * 128, (pair + 1) * 128)
        gctx_turned, qu_turned, qv_turned = gctx[:, cols].T, qu[:, cols].T, qv[:, cols].T
        gqu, gqv = [], []
        for h in range(2):
            own = slice(64 * h, 64 * h + 64)
            rows = slice(pair * 128 + 64 * h, pair * 128 + 64 * h + 64)
            pr = probs[2 * pair + h]
            gc = jnp.where(head_mask(h, count), gctx[:, cols], zero)
            gprobs = dot_nt(gc, v[:, cols])
            gv_turned[rows, :] = dot_nn(gctx_turned[own], pr).astype(BF16)
            weighted = pr.astype(F32) * gprobs
            gs = weighted - pr.astype(F32) * jnp.sum(weighted, axis=1, keepdims=True)
            gs = gs.astype(BF16)
            gqu.append(dot_nn(gs, k[:, cols]))
            gk_turned[rows, :] = (dot_nn(qu_turned[own], gs) * scale).astype(BF16)
            turned = dot_nn(gs, mirror)
            wide = jnp.concatenate([turned, jnp.zeros((count, count), F32)], axis=1)
            wide = pltpu.roll(wide, 0, 1, stride=1, stride_axis=0).astype(BF16)
            gqv.append(dot_nn(wide, pk[:, cols]))
            gpk_turned[rows, :] = (dot_nn(qv_turned[own], wide) * scale).astype(BF16)
        a = jnp.where(first, gqu[0], gqu[1]) * scale
        b = jnp.where(first, gqv[0], gqv[1]) * scale
        gvec_o[3:4, cols] = rows_sum(a)
        gvec_o[4:5, cols] = rows_sum(b)
        gq[:, cols] = (a + b).astype(BF16)
    gk, gv = gk_turned[...].T, gv_turned[...].T
    gvec_o[1:2, :] = rows_sum(gq[...].astype(F32))
    gvec_o[2:3, :] = rows_sum(gv.astype(F32))
    dw[0] = dot_tn(gq[...], na[...]).astype(BF16)
    dw[1] = dot_nn(gk_turned[...], na[...]).astype(BF16)
    dw[2] = dot_nn(gv_turned[...], na[...]).astype(BF16)
    dw[3] = dot_nn(gpk_turned[...], table[...]).astype(BF16)
    io.wait(0, 12, 13, 14, 15)
    gm = gmix[...].T
    for part in range(3):
        cols = slice(part * 512, (part + 1) * 512)
        gated = (zr[:, cols].astype(F32) * c[:, cols].astype(F32)).astype(BF16)
        dw[5 + part] = dot_nn(gm, gated).astype(BF16)
    emit(
        place(exact), keep, send, 128, lambda start, count, part: dw[part, pl.ds(start, count), :],
        32, [(part, 0, 32, part // 4, part % 4 * 32) for part in range(8)],
    )
    io.ship(1, 2)
    total = dot_nt(gq[...], w4[0]) + dot_nt(gk, w4[1]) + dot_nt(gv, w4[2])
    u = y1[...].astype(BF16).astype(F32)
    hat, inv = normalize(u)
    ggain_o[...] = rows_sum(total * hat)
    gvec_o[0:1, :] = rows_sum(total)
    gu_o[...] = normalize_back(total * gain[...], hat, inv)


def lane_piece(source, start, count):
    block, away = start // 128 * 128, start % 128
    wide = 128 if away + count <= 128 else 256
    value = source[:, block : block + wide]
    if away:
        value = pltpu.roll(value, wide - away, 1)
    return value


def pack_small(put, v512, v1024, v1536, v_rest, b1, b_in, packed):
    lane = lax.broadcasted_iota(jnp.int32, (32, 128), 1)
    row = lax.broadcasted_iota(jnp.int32, (32, 128), 0)
    for which in range(16):
        first = lane_piece(v512, 32 * which, 32)
        second = pltpu.roll(lane_piece(v1024, 64 * which, 64), 32, 1)
        third = lane_piece(v1536, 96 * which, 96)[:, :128]
        rest = lane_piece(v_rest, 96 * which, 96)[:, :128]
        bias = lane_piece(b_in, 192 * which, 192)
        rows = pl.ds(32 * which, 32)
        packed[rows, 0:128] = jnp.where(lane < 32, first, second).astype(BF16)
        packed[rows, 128:256] = third.astype(BF16)
        packed[rows, 256:384] = jnp.where(row < 8, rest, bias[:, :128]).astype(BF16)
        packed[rows, 384:512] = jnp.where(row < 8, b1[:, 128 * which : 128 * (which + 1)], bias[:, 128:]).astype(BF16)
    put(
        lambda start, count, part: packed[pl.ds(start, count), :],
        32, [(0, 0, 16, 0, 128), (0, 16, 16, 1, 128)],
    )


def last_kernel(
    exact, io, frames, p_in, g2, gu_a, gu_m, w1, w2, gains, shifts,
    gb1_r, ggain_r, gshift_r, gtaps_r, gmshift, gagain, gavec, gbin_0, gbin_1, gmgain, gmshift_0, gmshift_1,
    gggain, ggshift_0, ggshift_1, ggtaps_0, ggtaps_1,
    gx_o, keep, send, a, dw, v512, v1024, v1536, v_rest, b1, b_in, packed, hidden_sum,
):
    put = functools.partial(emit, place(exact), keep, send, 144)
    for ref in (v512, v1024, v_rest, b1, b_in):
        ref[...] = jnp.zeros(ref.shape, F32)
    v512[1:3, :] = ggain_r[...]
    v512[5:9, :] = gshift_r[...]
    v512[9:10, :] = gagain[...]
    v512[10:16, :] = gavec[...]
    v512[16:17, :] = gmgain[...]
    v512[17:18, :] = gmshift_0[...]
    v512[18:19, :] = gmshift_1[...]
    v1024[0:31, :] = gtaps_r[...]
    v1024[31:32, :] = gmshift[...]
    part_width = ggtaps_0.shape[1]
    v1536[0:31, :part_width] = ggtaps_0[...]
    v1536[0:31, part_width:] = ggtaps_1[...]
    v1536[31:32, :] = gggain[...]
    v_rest[0:1, :] = ggshift_0[...]
    v_rest[1:2, :] = ggshift_1[...]
    b1[1:2, :] = gb1_r[...]
    half = gbin_0.shape[1]
    b_in[8:9, :half] = gbin_0[...]
    b_in[8:9, half:] = gbin_1[...]

    g1 = g2[...] + gu_a[...] + gu_m[...]
    x = frames[...].astype(F32)
    hat, inv = normalize(x)
    n = (hat * gains[0:1, :] + shifts[0:1, :]).astype(BF16)
    io.wait(1)
    for c in range(a.shape[1] // 512):
        cols = slice(c * 512, (c + 1) * 512)
        h = p_in[:, cols]
        a[:, cols] = (h * sigmoid(h)).astype(BF16)
    gf = (0.5 * g1).astype(BF16)
    v512[4:5, :] = rows_sum(gf.astype(F32))
    io.wait(5, 6)
    g_hid = hidden_back(put, n, gf, p_in, a, w1, w2, hidden_sum, dw)
    b1[0:1, :] = hidden_sum[...]
    v512[0:1, :] = rows_sum(g_hid * hat)
    v512[3:4, :] = rows_sum(g_hid)
    pack_small(put, v512, v1024, v1536, v_rest, b1, b_in, packed)
    io.ship(1, 2)
    gx_o[...] = g1 + normalize_back(g_hid * gains[0:1, :], hat, inv)


def add_core_x(rows, io, keep, got, stay, away):
    io.wait(0, 1)
    add_rows(away, 0, 8 * rows, (keep, 8 * rows), (got, 8 * rows))
    spare = away.shape[0] - 8 * rows
    away[pl.ds(8 * rows, spare), :] = jnp.zeros((spare, 512), BF16)
    io.ship(1)
    add_rows(stay, 0, 8 * rows, (keep, 0), (got, 0))


def tail_a_kernel(rows_f, io, keep_f, got_f, f_0, f_1, f_2, f_3):
    for at, ref in ((2, f_2), (1, f_1), (3, f_3), (0, f_0)):
        add_rows(ref, 0, 4 * rows_f, (keep_f, at * 4 * rows_f), (got_f, at * 4 * rows_f))
        io.ship(at)


def tail_b_kernel(rows_m, rows_a, io, keep_m, got_m, stay_a, got_a, m_0, m_1, m_2, m_3, stay, away):
    io.wait(2, 3)
    for odd, ref in ((1, away), (0, stay)):
        for high in range(2):
            for y in range(2):
                first = (y * 4 + 2 * high + odd) * rows_a
                add_rows(ref, (2 * high + y) * rows_a, rows_a, (stay_a, first), (got_a, first))
        io.ship(4 + odd)
    io.wait(0, 1)
    for at, ref in ((2, m_2), (1, m_1), (3, m_3), (0, m_0)):
        add_rows(ref, 0, 4 * rows_m, (keep_m, at * 4 * rows_m), (got_m, at * 4 * rows_m))
        io.ship(at)


def tail_c_kernel(rows_f, rows_a, io, f_0, f_1, f_2, f_3, stay, got, f_stay, f_away, z_stay, z_away):
    for odd, ref in ((1, f_away), (0, f_stay)):
        for high in range(2):
            first = (2 * high + odd) * rows_f
            add_rows(ref, high * rows_f, rows_f, *[(term, first) for term in (f_0, f_1, f_2, f_3)])
        io.ship(odd)
    for high, ref in ((1, z_away), (0, z_stay)):
        add_rows(ref, 0, 2 * rows_a, (stay, high * 2 * rows_a), (got, high * 2 * rows_a))
        io.ship(2 + high)


def tail_d_kernel(
    rows_m, rows_f, rows_a, io, m_0, m_1, m_2, m_3, f_stay, f_got, z_stay, z_got,
    z_0, z_1, z_2, z_3, f_0, f_1, a_0, a_1,
):
    for at, ref in ((1, z_1), (2, z_2), (3, z_3), (0, z_0)):
        add_rows(ref, 0, rows_m, *[(term, at * rows_m) for term in (m_0, m_1, m_2, m_3)])
        io.ship(at)
    for high, ref in ((1, f_1), (0, f_0)):
        add_rows(ref, 0, rows_f, (f_stay, high * rows_f), (f_got, high * rows_f))
        io.ship(4 + high)
    for y, ref in ((1, a_1), (0, a_0)):
        add_rows(ref, 0, rows_a, (z_stay, y * rows_a), (z_got, y * rows_a))
        io.ship(6 + y)


def tail_e_kernel(rows_m, rows_f, rows_a, io, m_0, m_1, m_2, m_3, f_0, f_1, a_0, a_1, out):
    add_rows(out, 0, rows_m, (m_0, 0), (m_1, 0), (m_2, 0), (m_3, 0))
    add_rows(out, rows_m, rows_a, (a_0, 0), (a_1, 0))
    add_rows(out, rows_m + rows_a, rows_f, (f_0, 0), (f_1, 0))


def finish_kernel(
    io, side, r_own, r_far, own, far,
    ffn_in_o, b1_o, ffn_out_o, gains_o, shifts_o, m_taps_o, m_shift_o, merge_o, attn_o, attn_out_o, a_gain_o, a_vec_o,
    mlp_in_o, b_in_o, mlp_out_o, m_gain_o, m_shifts_o, g_gain_o, g_shifts_o, g_taps_o, small,
):
    def half(which, first, count, cols=slice(0, 512)):
        rows = slice(first, first + count)
        return jnp.where(side[0] == which, own[rows, cols], far[rows, cols]).astype(F32)

    def pair(first, count, cols=slice(0, 512)):
        rows = slice(first, first + count)
        return r_own[rows, cols].astype(F32) + r_far[rows, cols].astype(F32)

    def span(start, count):
        return slice(start, start + count)

    io.wait(1, 2)
    for q in range(4):
        cols = span(128 * q, 128)
        ffn_in_o[1, cols, :] = pair(0, 128, cols)
        ffn_out_o[1, :, span(512 * q, 512)] = pair(128 + 32 * q, 32)
    for part in range(2):
        merge_o[:, span(512 * part, 512)] = pair(256 + 32 * part, 32)
    io.ship(7)
    io.wait(3, 4)
    for q in range(4):
        cols = span(128 * q, 128)
        ffn_in_o[0, cols, :] = half(0, 224, 128, cols)
        ffn_out_o[0, :, span(512 * q, 512)] = half(1, 224 + 32 * q, 32)
    io.ship(0, 2)
    for part in range(2):
        mlp_in_o[span(96 * part, 96), :] = half(part, 0, 96)
        small[span(16 * part, 16), :] = half(part, 352, 16)
    for q in range(4):
        attn_o[q] = half(0, 96 + 32 * q, 32)
    attn_out_o[...] = half(1, 96, 32)
    for part in range(3):
        mlp_out_o[:, span(512 * part, 512)] = half(1, 128 + 32 * part, 32)
    io.ship(8, 9, 12, 14)
    first = small[:, 0:128]
    gains_o[...] = first[0:3, 0:32]
    shifts_o[...] = first[3:9, 0:32]
    a_gain_o[...] = first[9:10, 0:32].reshape(32)
    a_vec_o[...] = first[10:16, 0:32]
    m_gain_o[...] = first[16:17, 0:32].reshape(32)
    m_shifts_o[...] = first[17:19, 0:32]
    second = pltpu.roll(first, 96, 1)
    m_taps_o[...] = second[0:31, 0:64]
    m_shift_o[...] = second[31:32, 0:64].reshape(64)
    third = small[:, 128:256]
    g_taps_o[...] = third[0:31, 0:96]
    g_gain_o[...] = third[31:32, 0:96].reshape(96)
    g_shifts_o[...] = small[0:2, 256:352]
    b_in_o[...] = small[8:9, 256:448].reshape(192)
    b1_o[...] = small[0:2, 384:512]


ANY = pl.BlockSpec(memory_space=pl.ANY)


def shape(dims, kind=F32):
    return jax.ShapeDtypeStruct(dims, kind)


class Kernel:
    def __init__(self, copies_in, copies_out):
        self.copies_in, self.copies_out, self.shipped = copies_in, copies_out, set()

    def wait(self, *which):
        for at in which:
            for copy in self.copies_in[at]:
                copy.wait()

    def ship(self, *which):
        for at in which:
            self.shipped.add(at)
            for copy in self.copies_out[at]:
                copy.start()


def run(body, args, outs, scratch=(), late=(), smem=(), after=(), mib=63):
    arrays, reads, holds = [], [], []
    for at, arg in enumerate(args):
        if isinstance(arg, tuple):
            array, layer = arg
            reads.append([(len(arrays), layer, None)])
            arrays.append(array)
            dims, kind = array.shape[1:], array.dtype
        else:
            pieces = arg if isinstance(arg, list) else [arg]
            rows = sum(piece.shape[0] for piece in pieces)
            first, read = 0, []
            for piece in pieces:
                read.append((len(arrays), None, (first, piece.shape[0]) if len(pieces) > 1 else None))
                arrays.append(piece)
                first += piece.shape[0]
            reads.append(read)
            dims, kind = (rows,) + pieces[0].shape[1:], pieces[0].dtype
        holds.append((pltpu.SMEM if at in smem else pltpu.VMEM)(dims, kind))
    shapes, writes = [], []
    for out in outs:
        pieces = out if isinstance(out, list) else [out]
        first, write = 0, []
        for piece in pieces:
            write.append((len(shapes), (first, piece.shape[0]) if len(pieces) > 1 else None))
            shapes.append(piece)
            first += piece.shape[0]
        writes.append(write)
        dims = (first,) + pieces[0].shape[1:] if isinstance(out, list) else out.shape
        holds.append(pltpu.VMEM(dims, pieces[0].dtype))
    n_in, n_after, n_out, n_args = len(arrays), len(after), len(shapes), len(args)

    def kernel(*refs):
        sources, refs = refs[:n_in], refs[n_in + n_after :]
        targets, refs = refs[:n_out], refs[n_out:]
        held, refs = refs[: len(holds)], refs[len(holds) :]
        in_sems, out_sems, refs = refs[0], refs[1], refs[2:]

        def rows_of(ref, span):
            return ref if span is None else ref.at[pl.ds(*span)]

        copies_in = [
            [
                pltpu.make_async_copy(
                    sources[source] if layer is None else sources[source].at[layer], rows_of(held[at], span),
                    in_sems.at[source],
                )
                for source, layer, span in read
            ]
            for at, read in enumerate(reads)
        ]
        copies_out = [
            [
                pltpu.make_async_copy(rows_of(held[n_args + at], span), targets[target], out_sems.at[target])
                for target, span in write
            ]
            for at, write in enumerate(writes)
        ]
        early = [at for at in range(n_args) if at not in late]
        for at in early + list(late):
            for copy in copies_in[at]:
                copy.start()
        state = Kernel(copies_in, copies_out)
        state.wait(*early)
        body(state, *held, *refs)
        state.ship(*[at for at in range(len(outs)) if at not in state.shipped])
        for copies in copies_out:
            for copy in copies:
                copy.wait()

    return pl.pallas_call(
        kernel,
        out_shape=tuple(shapes),
        in_specs=[ANY] * (n_in + n_after),
        out_specs=(ANY,) * n_out,
        scratch_shapes=holds
        + [pltpu.SemaphoreType.DMA((n_in,)), pltpu.SemaphoreType.DMA((n_out,))]
        + list(scratch),
        compiler_params=pltpu.CompilerParams(vmem_limit_bytes=mib * MIB),
        cost_estimate=pl.CostEstimate(flops=1, bytes_accessed=1, transcendentals=0),
    )(*arrays, *after)


def swap(value, x=0, y=0, z=0, core=0):
    away = 16 * x + 4 * z + 2 * y + core
    return lax.ppermute(value, ("branch", "dp"), [(source, source ^ away) for source in range(32)])


def across_xy(parts):
    return [swap(parts[1], y=1), swap(parts[2], x=1), swap(parts[3], x=1, y=1)]


def across_z(parts):
    return [swap(parts[at], z=at) for at in (1, 2, 3)]


def local(frames, lengths, cotangent, *weights):
    (
        ffn_in, ffn_in_bias, ffn_out, shared_gains, shared_shifts, merge_kernel, merge_shift, merge_weight,
        attn_weights, attn_out, attn_gain, attn_vectors, mlp_in, mlp_in_bias, mlp_out, mlp_gain, mlp_shifts,
        gate_gain, gate_shifts, gate_kernel,
    ) = weights
    size = lax.axis_size("dp")
    exact = size == 16 and lax.axis_size("branch") == 2
    count, width = frames.shape
    hidden = ffn_in.shape[2]
    half = gate_gain.shape[0]
    taps = gate_kernel.shape[0]
    down, up = tables(count, width)
    act = lambda cols, kind=F32: shape((count, cols), kind)
    vmem = lambda dims, kind=BF16: pltpu.VMEM(dims, kind)
    line = lambda rows, cols: shape((rows, cols))
    rows16 = lambda rows: shape((rows, 512), BF16)
    cut = lambda *rows: [rows16(piece) for piece in rows]
    rows_r, rows_a, rows_m, rows_f = 320, 128, 96, 144
    spare = 384

    (
        y1, p1, low, high, na, qu, qv, k, v, probs, ctx, nm, slope, zr, c, hat, inv, activations, g2, e, joined, out_r,
        gb1_r, ggain_r, gshift_r, attn_gain, mlp_gain, gate_gain,
    ) = run(
        forward_kernel,
        (
            frames, lengths, cotangent, (ffn_in, 0), (ffn_in, 1), ffn_in_bias, (ffn_out, 0), (ffn_out, 1), shared_gains,
            shared_shifts, merge_kernel, merge_shift, merge_weight, attn_weights, attn_out, attn_gain, attn_vectors, mlp_in,
            mlp_in_bias, mlp_out, mlp_gain, mlp_shifts, gate_gain, gate_shifts, gate_kernel, down,
        ),
        (
            act(width), act(hidden), act(128, jnp.int32), act(128, jnp.int32), *(act(width, BF16),) * 5,
            shape((HEADS, count, count), BF16), act(width, BF16), act(width, BF16), act(2 * half, BF16), act(half, BF16),
            act(half, BF16), act(half, BF16), act(128), act(width, BF16), act(width), act(2 * width, BF16), act(2 * width),
            rows16(16 * rows_r), line(1, hidden), line(2, width), line(4, width),
            line(1, width), line(1, width), line(1, half),
        ),
        [
            vmem((count, width)), vmem((count, width)), vmem((2 * count, width)), vmem((count, count), F32),
            vmem((count, half)), vmem((count, half), F32), vmem((8, count + 32, half // 2), F32),
            vmem((taps, 8, half // 2), F32), vmem((count, hidden), F32), vmem((count, hidden)), vmem((512, hidden)),
            vmem((1, 2 * width), F32), vmem((1, 2 * half), F32),
        ],
        late=[FORWARD_IN.index(name) for name in FORWARD_LATER],
        smem=(1,),
    )
    if exact:
        r_own = lax.psum_scatter(out_r, "dp", scatter_dimension=0, tiled=True)
    gatt, gmix, gtaps_r, gmshift = run(
        merge_back_kernel,
        (g2, joined, merge_kernel, merge_weight, low, high),
        (act(width, BF16), act(width, BF16), line(taps, 2 * width), line(1, 2 * width)),
        [
            vmem((8, count + 32, 2 * width), F32), vmem((taps, 8, 2 * width), F32), vmem((taps, 8, 2 * width), F32),
            vmem((count, 2 * width), F32),
        ],
        late=(0, 3, 1, 4, 5),
    )
    gu_a, keep_a, send_a, gagain, gavec = run(
        functools.partial(attend_back_kernel, exact),
        (
            y1, gatt, up, na, qu, qv, k, v, probs, ctx, attn_weights, attn_out, attn_gain, gmix, zr, c,
        ),
        (act(width), rows16(16 * rows_a), rows16(16 * rows_a), line(1, width), line(6, width)),
        [
            vmem((2 * count, width)), vmem((count, width)), vmem((width, count)), vmem((width, count)),
            vmem((width, 2 * count)), vmem((count, width)), vmem((8, width, width)),
        ],
        late=(1, 9, 11, 2, 10, 8, 7, 6, 5, 4, 3, 13, 14, 15, 0, 12),
    )
    got_a = swap(send_a, core=1) if exact else None
    part_width = half // 2
    conv_scratch = [
        vmem((8, count + 32, part_width), F32), vmem((taps, 8, part_width), F32), vmem((taps, 8, part_width), F32),
        vmem((count, part_width), F32),
    ]
    gh, gc, gl, gbin_0, ggshift_1, ggtaps_0, gmshift_1 = run(
        gate_back_first_kernel,
        (gmix, slope, zr, c, hat, mlp_out, gate_gain, gate_shifts, gate_kernel, low, high),
        (
            act(half, BF16), act(part_width), act(part_width), line(1, half), line(1, half), line(taps, part_width),
            line(1, width),
        ),
        conv_scratch,
        late=(0, 5, 3, 2, 1, 4),
        after=[gu_a],
    )
    if exact:
        stay_a, away_a = run(
            functools.partial(add_core_x, rows_a), (keep_a, got_a), (rows16(8 * rows_a), rows16(8 * rows_a + spare)), late=(0, 1),
            after=[gh],
        )
        got_a = swap(away_a, x=1)
    gu_m, gh_second, gbin_1, gggain, ggshift_0, ggtaps_1, gmgain, gmshift_0 = run(
        gate_back_second_kernel,
        (
            gc, gl, slope, hat, inv, gate_gain, gate_shifts, gate_kernel, low, high, y1, gh, mlp_in, mlp_gain,
        ),
        (
            act(width), act(half, BF16), line(1, half), line(1, half), line(1, half), line(taps, part_width),
            line(1, width), line(1, width),
        ),
        conv_scratch + [vmem((count, part_width), F32)],
        late=(0, 3, 1, 2, 4, 10, 11, 12),
        after=[away_a] if exact else [],
    )
    g_frames, keep_f, *send_f = run(
        functools.partial(last_kernel, exact),
        (
            frames, p1, g2, gu_a, gu_m, (ffn_in, 0), (ffn_out, 0), shared_gains, shared_shifts,
            gb1_r, ggain_r, gshift_r, gtaps_r, gmshift, gagain, gavec, gbin_0, gbin_1, gmgain, gmshift_0, gmshift_1,
            gggain, ggshift_0, ggshift_1, ggtaps_0, ggtaps_1,
        ),
        (act(width), rows16(16 * rows_f), cut(1152, 1152)),
        [
            vmem((count, hidden)), vmem((512, hidden)), vmem((32, width), F32),
            vmem((32, 2 * width), F32),
            vmem((32, half), F32), vmem((32, half), F32), vmem((32, hidden), F32), vmem((32, 2 * half), F32),
            vmem((512, 512)), vmem((1, hidden), F32),
        ],
        late=(1, 6, 5),
    )
    got_f = [swap(piece, core=1) for piece in send_f] if exact else []
    keep_m, *send_m = run(
        functools.partial(gate_weights_kernel, exact),
        (gh, gh_second, nm),
        (rows16(16 * rows_m), cut(768, 768)),
        [vmem((2 * half, 512))],
        after=[g_frames],
    )
    if exact:
        got_m = [swap(piece, core=1) for piece in send_m]
        sums = lambda *rows: tuple(rows16(count) for count in rows)
        small = functools.partial(run, mib=40)
        f = run(
            functools.partial(tail_a_kernel, rows_f), (keep_f, got_f), sums(*(4 * rows_f,) * 4), after=[keep_m]
        )
        f = (f[0], *across_xy(f))
        *m, z_stay, z_away = run(
            functools.partial(tail_b_kernel, rows_m, rows_a),
            (keep_m, got_m, stay_a, got_a),
            sums(*(4 * rows_m,) * 4, 4 * rows_a, 4 * rows_a),
            late=(0, 1, 2, 3),
            after=[f[0]],
        )
        m = (m[0], *across_xy(m))
        f_stay, f_away, z_stay, z_away = small(
            functools.partial(tail_c_kernel, rows_f, rows_a),
            (*f, z_stay, swap(z_away, z=1)),
            sums(*(2 * rows_f,) * 2, *(2 * rows_a,) * 2),
        )
        r_far = swap(r_own, x=1)
        *m, f_stay, f_away, a_stay, a_away = small(
            functools.partial(tail_d_kernel, rows_m, rows_f, rows_a),
            (*m, f_stay, swap(f_away, z=1), z_stay, swap(z_away, z=2)),
            sums(*(rows_m,) * 4, rows_f, rows_f, rows_a, rows_a),
        )
        m = (m[0], *across_z(m))
        own, = small(
            functools.partial(tail_e_kernel, rows_m, rows_f, rows_a),
            (*m, f_stay, swap(f_away, z=2), a_stay, swap(a_away, y=1)),
            sums(rows_f + rows_a + rows_m),
            after=[r_far],
        )
        far = swap(own, x=1)
        side = lax.axis_index("branch").reshape(1).astype(jnp.int32)
        flat = lambda n: shape((n,))
        done = small(
            finish_kernel,
            (side, r_own, r_far, own, far),
            (
                shape((2, 512, 128)), line(2, 128), shape((2, 32, hidden)), line(3, 32), line(6, 32), line(taps, 64),
                flat(64), line(32, 2 * width), shape((4, 32, width)), line(32, width), flat(32), line(6, 32),
                line(192, width), flat(192), line(32, half), flat(32), line(2, 32), flat(96), line(2, 96),
                line(taps, 96),
            ),
            [vmem((32, 512), F32)],
            smem=(0,),
            late=(1, 2, 3, 4),
        )
        turned = {2, 7, 8, 9, 12, 14}
        done = [jnp.swapaxes(v, -1, -2) if at in turned else v for at, v in enumerate(done)]
    else:

        def scatter(value):
            part = lax.psum_scatter(value, "dp", scatter_dimension=0, tiled=True)
            return lax.psum(part, "branch").T

        def out_rows(rows):
            parts = rows.shape[1] // 32
            return rows.reshape(16, parts, 32, 512).transpose(0, 2, 1, 3).reshape(512, 512 * parts)

        def columns(rows):
            return rows.reshape(16, 128, 4, 128).transpose(0, 3, 2, 1).reshape(2048, 512)

        def pieces(rows, per):
            return rows[:, :, :per].transpose(1, 0, 2).reshape(rows.shape[1], 16 * per)

        def ordered(keep, send, rows):
            both = jnp.stack([keep.reshape(2, 2, 4, rows, 512), send.reshape(2, 2, 4, rows, 512)], axis=3)
            return both.astype(F32).transpose(2, 1, 3, 0, 4, 5).reshape(16, 2, rows, 512)

        r = out_r.astype(F32).reshape(16, 320, 512)
        a, m, f = [
            ordered(*group)
            for group in (
                (keep_a, send_a, rows_a),
                (keep_m, jnp.concatenate(send_m), rows_m), (keep_f, jnp.concatenate(send_f), rows_f),
            )
        ]
        small = jnp.concatenate([f[:, 0, 128:], f[:, 1, 128:]], axis=1)
        vectors = pieces(small[:, 0:19], 32)
        m_both, g_both = pieces(small[:, :, 32:], 64), pieces(small[:, :, 128:], 96)
        done = [
            jnp.stack([scatter(columns(v)) for v in (f[:, 0, :128], r[:, :128])]),
            pieces(small[:, 0:2, 384:], 128),
            jnp.stack([scatter(out_rows(v)) for v in (f[:, 1, :128], r[:, 128:256])]),
            vectors[0:3], vectors[3:9], m_both[:31], m_both[31],
            scatter(out_rows(r[:, 256:])),
            jnp.stack([scatter(out_rows(a[:, 0, 32 * i : 32 * i + 32])) for i in range(4)]),
            scatter(out_rows(a[:, 1, :32])),
            vectors[9], vectors[10:16],
            scatter(m.reshape(3072, 512)),
            pieces(small[:, 8:9, 256:], 192)[0],
            scatter(out_rows(a[:, 1, 32:])),
            vectors[16], vectors[17:19], g_both[31], pieces(small[:, 0:2, 256:], 96), g_both[:31],
        ]
        for at, v in enumerate(done):
            if at not in (0, 2, 7, 8, 9, 12, 14):
                part = lax.psum_scatter(v, "dp", scatter_dimension=v.ndim - 1, tiled=True)
                done[at] = lax.psum(part, "branch")
    return (activations, g_frames) + tuple(done)


def solution(mesh):
    rows = P(("branch", "dp"), None)
    last = {1: P("dp"), 2: P(None, "dp"), 3: P(None, None, "dp")}
    ranks = (3, 2, 3, 2, 2, 2, 1, 2, 3, 2, 1, 2, 2, 1, 2, 1, 2, 1, 2, 2)
    return jax.shard_map(
        local,
        mesh=mesh,
        in_specs=(rows,) * 3 + (P(),) * 20,
        out_specs=(rows, rows) + tuple(last[r] for r in ranks),
        check_vma=False,
    )
```
